32 devices in a mesh: group: 4 (over y, x), member: 8 (over z, core).
Axes of the slice: x: 2, y: 2, z: 4, core: 2. Of those that a mesh axis runs over, the one named last changes fastest.
Arguments:
- points: bfloat16 [8192, 768], P(('group', 'member')), may hold values from -9 to 9
- centroids: bfloat16 [8192, 768], P('group'), may hold values from -5 to 5
- dest_group: int32 [8192, 1], P(('group', 'member')), may hold values from 0 to 3; in each aligned block of 256 rows (0 to 255, 256 to 511, ...) at most 64 rows name the same one
Outputs:
- refined: bfloat16 [8192, 768], P(('group', 'member'))
The draws below stay inside these ranges and needn't reach their ends.
Inputs may be any that keep to these rules, and one draw needn't show every extreme that they name: `dest_group`: among the 256 rows of one device, at most 64 name the same group, a bound that some block reaches of them.
All inputs are finite; a program needn't handle non-finite values.
Results may differ from the reference program's by a relative error of at most 0.0025.
Values may be sent and summed in bfloat16 or wider, within the bound.
No kernel may reach another device: no remote copies, remote signals or barrier semaphores. Data moves between devices by JAX's collectives and lax.ppermute only.
A program may use at most 64 MiB of HBM per device.

```python
import math
import jax
import jax.numpy as jnp
import numpy as np
from jax import lax

D = 768
FINE = 2048
PTS_DEV = 256
CAP = 64
POINTS = 8192
CENTS = 8192
N_GROUP = 4
N_MEMBER = 8


def draw_centroids(key, part):
    values = jnp.clip(jax.random.normal(jax.random.fold_in(key, 11), (CENTS, D), jnp.float32), -5.0, 5.0)
    return values.astype(jnp.bfloat16)


def draw_points(key, part):
    values = jnp.clip(jax.random.normal(jax.random.fold_in(key, 12), (POINTS, D), jnp.float32), -5.0, 5.0)
    return values.astype(jnp.bfloat16)


def routed_block(rng, own, number, rows, amount, top, bound, skew):
    ranking = jax.random.permutation(rng, amount)
    crowded, common = shares(amount, rows * top, bound, skew, True), shares(amount, rows * top, bound, skew, False)
    places = jnp.arange(amount)

    def named(sizes, turn):
        used = int((sizes > 0).sum())
        fixed = max(1, used // 4)
        shifted = fixed + (places - fixed + turn * (used - fixed)) % max(1, amount - fixed)
        return jnp.zeros((amount,), jnp.int32).at[ranking[jnp.where(places < fixed, places, shifted)]].set(jnp.asarray(sizes, jnp.int32))

    sizes = jnp.where(number % 4 == 0, named(crowded, number // 4), named(common, number - number // 4 - 1))
    mixed = jax.random.permutation(jax.random.fold_in(own, 3), amount)
    giver, taker = mixed[0:amount // 2 * 2:2], mixed[1:amount // 2 * 2:2]
    slack = jnp.minimum(sizes[giver] - 1, bound - sizes[taker]) // 2
    slack = jnp.where((giver == ranking[0]) | (taker == ranking[0]) | (sizes[taker] == 0), 0, jnp.maximum(slack, 0))
    shifted = jax.random.randint(jax.random.fold_in(own, 4), (amount // 2,), 0, 1 << 20) % (slack + 1)
    sizes = sizes.at[giver].add(-shifted).at[taker].add(shifted)
    items = jnp.searchsorted(jnp.cumsum(sizes), jnp.arange(rows * top), side="right").astype(jnp.int32)
    listing = items.reshape(top, rows).T
    listing = listing[jax.random.permutation(jax.random.fold_in(own, 1), rows)]
    turn = jax.random.randint(jax.random.fold_in(own, 2), (rows, 1), 0, top)
    return jnp.take_along_axis(listing, (jnp.arange(top)[None, :] + turn) % top, axis=1)


def shares(count, total, reach, lean, full):
    portions = [(1 << 20) // math.isqrt(standing ** lean) + 1 for standing in range(1, count + 1)]
    largest = reach if full else min(reach, max(-(-total // count), total * portions[0] // sum(portions)))
    least = 1 if total - largest >= count - 1 else 0
    given, rest = [largest] + [least] * (count - 1), total - largest - least * (count - 1)
    while rest > 0:
        free = [i for i in range(1, count) if given[i] < largest] or [i for i in range(1, count) if given[i] < reach]
        whole, left = sum([portions[i] for i in free]), rest
        for i in free:
            addition = min(reach - given[i], max(1, left * portions[i] // whole), rest)
            given[i] = given[i] + addition
            rest = rest - addition
    return np.array(given)


def setup_inputs(seed: int = 0) -> dict:
    splits = jax.random.split(jax.random.key(seed), 4)
    points = draw_points(jax.random.fold_in(splits[3], 71), 0)
    centroids = draw_centroids(jax.random.fold_in(splits[3], 71), 0)
    dest_group_keys = jax.random.split(jax.random.fold_in(splits[2], 1), POINTS // PTS_DEV)
    dest_group_turns = jax.random.permutation(jax.random.fold_in(splits[2], 3), POINTS // PTS_DEV)
    dest_group = jax.vmap(lambda own, number: routed_block(jax.random.fold_in(splits[2], 2), own, number, PTS_DEV, N_GROUP, 1, CAP, 2))(dest_group_keys, dest_group_turns).reshape((POINTS, 1))
    return {"points": points, "centroids": centroids, "dest_group": dest_group}


score_scale = 0.15


def reference(points, centroids, dest_group):
    destination = dest_group[:, 0].astype(jnp.int32)
    order = jnp.argsort(destination, stable=True).astype(jnp.int32)
    sorted_points = points[order]
    group_rows = N_GROUP * N_MEMBER * CAP
    block_rows = N_GROUP * CAP
    padded = jnp.concatenate([sorted_points, jnp.zeros((group_rows, D), points.dtype)], axis=0)
    per_group = jnp.sum((destination[None, :] == jnp.arange(N_GROUP, dtype=jnp.int32)[:, None]).astype(jnp.int32), axis=1).astype(jnp.int32)
    starts = (jnp.cumsum(per_group) - per_group).astype(jnp.int32)

    def refit(group_index):
        table = lax.dynamic_slice_in_dim(centroids, (group_index * FINE).astype(jnp.int32), FINE, 0)
        table_f = table.astype(jnp.float32)
        norms = jnp.sum(table_f * table_f, axis=1)
        start = starts[group_index]
        count = per_group[group_index]

        def step(carry, block_index):
            sums, counts = carry
            offset = (block_index * block_rows).astype(jnp.int32)
            rows = lax.dynamic_slice_in_dim(padded, (start + offset).astype(jnp.int32), block_rows, 0)
            valid = ((offset + jnp.arange(block_rows, dtype=jnp.int32)) < count).astype(jnp.float32)
            scores = score_scale * (jnp.dot(rows, table.T, preferred_element_type=jnp.float32) - 0.5 * norms[None, :])
            weights = (jax.nn.softmax(scores, axis=-1) * valid[:, None]).astype(jnp.bfloat16)
            sums = sums + jnp.dot(weights.T, rows, preferred_element_type=jnp.float32)
            counts = counts + jnp.sum(weights.astype(jnp.float32), axis=0)
            return (sums, counts), None

        init = (jnp.zeros((FINE, D), jnp.float32), jnp.zeros((FINE,), jnp.float32))
        (sums, counts), _ = lax.scan(step, init, jnp.arange(group_rows // block_rows, dtype=jnp.int32))
        return ((sums + table_f) / (counts + 1.0)[:, None]).astype(jnp.bfloat16)

    result = lax.map(refit, jnp.arange(N_GROUP, dtype=jnp.int32))
    return result.reshape(CENTS, D)
```

```python
import functools

import jax
import jax.numpy as jnp
from jax import lax
from jax.experimental import pallas as pl
from jax.experimental.pallas import tpu as pltpu
from jax.sharding import PartitionSpec as P

score_scale = 0.15
lanes = 128
vmem_limit = 48 * 1024 * 1024


def general(points, centroids, dest_group):
    group_count = lax.axis_size("group")
    member_count = lax.axis_size("member")
    point_rows = points.shape[0]
    capacity = point_rows // 4
    feature_dim = points.shape[1]
    fine_count = centroids.shape[0]
    destination = dest_group[:, 0]
    in_group = (destination[:, None] == jnp.arange(group_count, dtype=jnp.int32)[None, :]).astype(
        jnp.int32
    )
    earlier = jnp.cumsum(in_group, axis=0) - in_group
    own_rank = jnp.sum(earlier * in_group, axis=1)
    slot_index = destination * capacity + own_rank
    placement = (
        jnp.arange(group_count * capacity, dtype=jnp.int32)[:, None] == slot_index[None, :]
    ).astype(jnp.bfloat16)
    packed = jnp.dot(placement, points, preferred_element_type=jnp.float32).astype(jnp.bfloat16)
    packed = packed.reshape(group_count, capacity, feature_dim)
    slot_flags = jnp.dot(
        placement, jnp.ones((point_rows, 1), jnp.bfloat16), preferred_element_type=jnp.float32
    )
    slot_flags = slot_flags.astype(jnp.bfloat16).reshape(group_count, capacity, 1)
    centroid_f = centroids.astype(jnp.float32)
    centroid_norms = jnp.sum(centroid_f * centroid_f, axis=1)
    arrived, marks = (
        lax.all_to_all(packed, "group", split_axis=0, concat_axis=0, tiled=True),
        lax.all_to_all(slot_flags, "group", split_axis=0, concat_axis=0, tiled=True),
    )
    rows = arrived.reshape(-1, feature_dim)
    scores = score_scale * (
        jnp.dot(rows, centroids.T, preferred_element_type=jnp.float32)
        - 0.5 * centroid_norms[None, :]
    )
    weights = jax.nn.softmax(scores, axis=-1) * marks.reshape(-1, 1).astype(jnp.float32)
    responsibility = weights.astype(jnp.bfloat16).reshape(
        arrived.shape[0], arrived.shape[1], fine_count
    )
    all_rows = arrived.reshape(-1, feature_dim)
    all_weights = responsibility.reshape(-1, fine_count)
    weighted = jnp.dot(all_weights.T, all_rows, preferred_element_type=jnp.float32)
    soft_counts = jnp.dot(
        jnp.ones((1, all_weights.shape[0]), jnp.bfloat16),
        all_weights,
        preferred_element_type=jnp.float32,
    )[0]
    member_index = lax.axis_index("member")
    tile_sums, tile_counts = (
        lax.psum_scatter(weighted, "member", scatter_dimension=0, tiled=True),
        lax.psum_scatter(soft_counts, "member", scatter_dimension=0, tiled=True),
    )
    tile_rows = fine_count // member_count
    old_tile = lax.dynamic_slice_in_dim(centroid_f, member_index * tile_rows, tile_rows, 0)
    refined = ((tile_sums + old_tile) / (tile_counts + 1.0)[:, None]).astype(jnp.bfloat16)
    return refined


def vmem():
    return pl.BlockSpec(memory_space=pltpu.VMEM)


def smem():
    return pl.BlockSpec(memory_space=pltpu.SMEM)


def pack_kernel(place, dest, points, *packed):
    count = len(packed)
    row_count = points.shape[0]
    capacity = row_count // count
    apart = jnp.bitwise_xor(dest[...], place[0])
    lane = lax.broadcasted_iota(jnp.int32, (row_count, lanes), 1)
    named = (apart == lane).astype(jnp.float32)
    row_at = lax.broadcasted_iota(jnp.int32, (row_count, row_count), 0)
    col_at = lax.broadcasted_iota(jnp.int32, (row_count, row_count), 1)
    before = (col_at < row_at).astype(jnp.bfloat16)
    earlier = jnp.dot(before, named.astype(jnp.bfloat16), preferred_element_type=jnp.float32)
    rank = jnp.sum(earlier * named, axis=1, keepdims=True)
    slot = apart * capacity + rank.astype(jnp.int32)
    placement = (slot == col_at).astype(jnp.float32).T.astype(jnp.bfloat16)
    rows = jnp.dot(placement, points[...], preferred_element_type=jnp.float32)
    rows = rows.astype(jnp.bfloat16)
    for k in range(count):
        packed[k][...] = rows[k * capacity : (k + 1) * capacity]


def pack(place, dest_group, points, group_count):
    row_count, feature_dim = points.shape
    capacity = row_count // group_count
    return pl.pallas_call(
        pack_kernel,
        out_shape=[jax.ShapeDtypeStruct((capacity, feature_dim), points.dtype)] * group_count,
        in_specs=[smem(), vmem(), vmem()],
        out_specs=[vmem()] * group_count,
        compiler_params=pltpu.CompilerParams(vmem_limit_bytes=vmem_limit),
        cost_estimate=pl.CostEstimate(
            flops=4 * row_count * row_count * feature_dim,
            bytes_accessed=4 * row_count * feature_dim,
            transcendentals=0,
        ),
        name="pack",
    )(place, dest_group, points)


def soft_weights(rows, table, half_norms, scores, tile, first, inverse_at):
    fine_count = table.shape[0]
    row_count = rows.shape[0]
    dims = (((1,), (1,)), ((), ()))

    def score(index, top):
        at = pl.ds(pl.multiple_of(index * tile, tile), tile)
        block = lax.dot_general(
            table[at, :], rows[...], dims, preferred_element_type=jnp.float32
        )
        block = block - half_norms[at, :]
        scores[at, :] = block
        return jnp.maximum(top, jnp.max(block, axis=0, keepdims=True))

    top = lax.fori_loop(
        0, fine_count // tile, score, jnp.full((1, row_count), -jnp.inf, jnp.float32)
    )

    def total(index, sofar):
        at = pl.ds(pl.multiple_of(index * tile, tile), tile)
        block = jnp.exp(score_scale * (scores[at, :] - top))
        return sofar + jnp.sum(block, axis=0, keepdims=True)

    sofar = lax.fori_loop(
        0, fine_count // tile, total, jnp.zeros((1, row_count), jnp.float32)
    )
    return top, 1.0 / sofar


def tile_weights(scores, top, inverse, start, tile):
    at = pl.ds(pl.multiple_of(start, tile), tile)
    return (jnp.exp(score_scale * (scores[at, :] - top)) * inverse).astype(jnp.bfloat16)


def gather_rows(parts, rows):
    start = 0
    for part in parts:
        rows[start : start + part.shape[0], :] = part[...]
        start += part.shape[0]


def add_tile(weights, rows, sums, fresh):
    feature_dim = rows.shape[1]
    product = jnp.dot(weights, rows[...], preferred_element_type=jnp.float32)
    count = jnp.sum(weights.astype(jnp.float32), axis=1, keepdims=True)
    count = jnp.broadcast_to(count, (count.shape[0], lanes))
    if fresh:
        sums[:, :feature_dim] = product
        sums[:, feature_dim:] = count
    else:
        sums[:, :feature_dim] += product
        sums[:, feature_dim:] += count


def own_kernel(tile, parts_n, place, table, *refs):
    parts, (keep, give, half_norms, rows, scores) = refs[:parts_n], refs[parts_n:]

    @pl.loop(0, table.shape[0] // tile)
    def _(index):
        at = pl.ds(pl.multiple_of(index * tile, tile), tile)
        block = table[at, :].astype(jnp.float32)
        half_norms[at, :] = 0.5 * jnp.sum(block * block, axis=1, keepdims=True)

    gather_rows(parts, rows)
    top, inverse = soft_weights(rows, table, half_norms, scores, tile, None, None)
    mine, other = place[1] * tile, place[2] * tile
    add_tile(tile_weights(scores, top, inverse, mine, tile), rows, keep, True)
    add_tile(tile_weights(scores, top, inverse, other, tile), rows, give, True)


def step_kernel(tile, parts_n, place, table, half_norms, keep_in, give_in, *refs):
    parts, (keep, give, rows, scores) = refs[:parts_n], refs[parts_n:]
    keep[...] = keep_in[...]
    give[...] = give_in[...]

    @pl.when(place[0] == 1)
    def _():
        gather_rows(parts, rows)
        top, inverse = soft_weights(rows, table, half_norms, scores, tile, None, None)
        mine, other = place[1] * tile, place[2] * tile
        add_tile(tile_weights(scores, top, inverse, mine, tile), rows, keep, False)
        add_tile(tile_weights(scores, top, inverse, other, tile), rows, give, False)


def last_kernel(tile, parts_n, place, table, half_norms, keep, got, *refs):
    parts, passed = refs[:parts_n], refs[parts_n : 2 * parts_n]
    refined, rows, scores, sums = refs[2 * parts_n :]
    feature_dim = rows.shape[1]
    sums[...] = keep[...] + got[...]
    mine = place[1] * tile

    @pl.when(place[0] == 1)
    def _():
        gather_rows(parts, rows)

    @pl.when(place[0] == 2)
    def _():
        gather_rows(passed, rows)

    @pl.when(place[0] > 0)
    def _():
        top, inverse = soft_weights(rows, table, half_norms, scores, tile, None, None)
        add_tile(tile_weights(scores, top, inverse, mine, tile), rows, sums, False)

    old = table[pl.ds(pl.multiple_of(mine, tile), tile), :].astype(jnp.float32)
    scale = 1.0 / (sums[:, feature_dim : feature_dim + 1] + 1.0)
    refined[...] = ((sums[:, :feature_dim] + old) * scale).astype(jnp.bfloat16)


def cost(fine_count, row_count, feature_dim):
    return pl.CostEstimate(
        flops=4 * fine_count * row_count * feature_dim,
        bytes_accessed=2 * fine_count * feature_dim + 8 * row_count * feature_dim,
        transcendentals=fine_count * row_count,
    )


def handoff(points, centroids, dest_group):
    group_count = lax.axis_size("group")
    member_count = lax.axis_size("member")
    depth = member_count // 2
    feature_dim = points.shape[1]
    fine_count = centroids.shape[0]
    tile = fine_count // member_count
    group = lax.axis_index("group")
    member = lax.axis_index("member")
    level, core = member // 2, member % 2

    def perm(x, pairs):
        return lax.ppermute(x, "member", pairs)

    def swap(x):
        return perm(x, [(i, i ^ 1) for i in range(member_count)])

    def onward(x, step):
        up = [(2 * z, 2 * z + 2) for z in range(step - 1, depth - 1)]
        down = [(2 * z + 3, 2 * z + 1) for z in range(0, depth - step)]
        return perm(x, up + down)

    def ints(*values):
        return jnp.stack([jnp.asarray(v, jnp.int32) for v in values])

    packed = pack(ints(group), dest_group, points, group_count)
    own = packed[0]
    fetched = [
        lax.ppermute(packed[k], "group", [(i, i ^ k) for i in range(group_count)])
        for k in range(1, group_count)
    ]
    own_far = jnp.concatenate(fetched, axis=0)
    near, far = [own, swap(own)], [own_far, swap(own_far)]
    chunks = near + far

    sums_shape = jax.ShapeDtypeStruct((tile, feature_dim + lanes), jnp.float32)
    params = pltpu.CompilerParams(vmem_limit_bytes=vmem_limit)

    def scratch(rows):
        return [
            pltpu.VMEM((rows, feature_dim), jnp.bfloat16),
            pltpu.VMEM((fine_count, rows), jnp.float32),
        ]

    mine, other = member, member + 1 - 2 * core
    mine_rows = points.shape[0]
    keep, give, half_norms = pl.pallas_call(
        functools.partial(own_kernel, tile, 2),
        out_shape=[sums_shape, sums_shape, jax.ShapeDtypeStruct((fine_count, 1), jnp.float32)],
        in_specs=[smem()] + [vmem()] * 3,
        out_specs=[vmem()] * 3,
        scratch_shapes=scratch(mine_rows),
        compiler_params=params,
        cost_estimate=cost(fine_count, mine_rows, feature_dim),
        name="own_rows",
    )(ints(1, mine, other), centroids, own, own_far)

    for step in range(1, depth):
        chunks = [onward(chunk, step) for chunk in chunks]
        if step == depth - 1:
            break
        valid = jnp.where(core == 0, level >= step, level <= depth - 1 - step)
        keep, give = pl.pallas_call(
            functools.partial(step_kernel, tile, len(chunks)),
            out_shape=[sums_shape, sums_shape],
            in_specs=[smem()] + [vmem()] * (4 + len(chunks)),
            out_specs=[vmem()] * 2,
            scratch_shapes=scratch(2 * mine_rows),
            input_output_aliases={3: 0, 4: 1},
            compiler_params=params,
            cost_estimate=cost(fine_count, 2 * mine_rows, feature_dim),
            name="step_rows",
        )(ints(valid, mine, other), centroids, half_norms, keep, give, *chunks)

    got = swap(give)
    passed = [swap(chunk) for chunk in chunks]
    receives = jnp.where(core == 0, level == depth - 1, level == 0)
    ends = jnp.logical_or(level == depth - 1, level == 0)
    mode = jnp.where(receives, 1, jnp.where(ends, 2, 0))
    return pl.pallas_call(
        functools.partial(last_kernel, tile, len(chunks)),
        out_shape=jax.ShapeDtypeStruct((tile, feature_dim), jnp.bfloat16),
        in_specs=[smem()] + [vmem()] * (4 + 2 * len(chunks)),
        out_specs=vmem(),
        scratch_shapes=scratch(2 * mine_rows)
        + [pltpu.VMEM((tile, feature_dim + lanes), jnp.float32)],
        compiler_params=params,
        cost_estimate=cost(fine_count, 2 * mine_rows, feature_dim),
        name="last_rows",
    )(ints(mode, mine, other), centroids, half_norms, keep, got, *chunks, *passed)


def solution(mesh):
    def local(points, centroids, dest_group):
        groups, members = mesh.shape["group"], mesh.shape["member"]
        if groups * (points.shape[0] // 4) == points.shape[0] and 6 <= members <= 16:
            return handoff(points, centroids, dest_group)
        return general(points, centroids, dest_group)

    return jax.shard_map(
        local,
        mesh=mesh,
        in_specs=(P(("group", "member"), None), P("group", None), P(("group", "member"), None)),
        out_specs=P(("group", "member"), None),
        check_vma=False,
    )
```

```python
import functools
import math

import jax
import jax.numpy as jnp
from jax import lax
from jax.experimental import pallas as pl
from jax.experimental.pallas import tpu as pltpu
from jax.sharding import PartitionSpec as P

score_scale = 0.15
lanes = 128
exponent_scale = score_scale * math.log2(math.e)
vmem_limit = 20 * 1024 * 1024


def general(points, centroids, dest_group):
    group_count = lax.axis_size("group")
    member_count = lax.axis_size("member")
    point_rows = points.shape[0]
    capacity = point_rows // 4
    feature_dim = points.shape[1]
    fine_count = centroids.shape[0]
    destination = dest_group[:, 0]
    in_group = (destination[:, None] == jnp.arange(group_count, dtype=jnp.int32)[None, :]).astype(
        jnp.int32
    )
    earlier = jnp.cumsum(in_group, axis=0) - in_group
    own_rank = jnp.sum(earlier * in_group, axis=1)
    slot_index = destination * capacity + own_rank
    placement = (
        jnp.arange(group_count * capacity, dtype=jnp.int32)[:, None] == slot_index[None, :]
    ).astype(jnp.bfloat16)
    packed = jnp.dot(placement, points, preferred_element_type=jnp.float32).astype(jnp.bfloat16)
    packed = packed.reshape(group_count, capacity, feature_dim)
    slot_flags = jnp.dot(
        placement, jnp.ones((point_rows, 1), jnp.bfloat16), preferred_element_type=jnp.float32
    )
    slot_flags = slot_flags.astype(jnp.bfloat16).reshape(group_count, capacity, 1)
    centroid_f = centroids.astype(jnp.float32)
    centroid_norms = jnp.sum(centroid_f * centroid_f, axis=1)
    arrived, marks = (
        lax.all_to_all(packed, "group", split_axis=0, concat_axis=0, tiled=True),
        lax.all_to_all(slot_flags, "group", split_axis=0, concat_axis=0, tiled=True),
    )
    rows = arrived.reshape(-1, feature_dim)
    scores = score_scale * (
        jnp.dot(rows, centroids.T, preferred_element_type=jnp.float32)
        - 0.5 * centroid_norms[None, :]
    )
    weights = jax.nn.softmax(scores, axis=-1) * marks.reshape(-1, 1).astype(jnp.float32)
    responsibility = weights.astype(jnp.bfloat16).reshape(
        arrived.shape[0], arrived.shape[1], fine_count
    )
    all_rows = arrived.reshape(-1, feature_dim)
    all_weights = responsibility.reshape(-1, fine_count)
    weighted = jnp.dot(all_weights.T, all_rows, preferred_element_type=jnp.float32)
    soft_counts = jnp.dot(
        jnp.ones((1, all_weights.shape[0]), jnp.bfloat16),
        all_weights,
        preferred_element_type=jnp.float32,
    )[0]
    member_index = lax.axis_index("member")
    tile_sums, tile_counts = (
        lax.psum_scatter(weighted, "member", scatter_dimension=0, tiled=True),
        lax.psum_scatter(soft_counts, "member", scatter_dimension=0, tiled=True),
    )
    tile_rows = fine_count // member_count
    old_tile = lax.dynamic_slice_in_dim(centroid_f, member_index * tile_rows, tile_rows, 0)
    refined = ((tile_sums + old_tile) / (tile_counts + 1.0)[:, None]).astype(jnp.bfloat16)
    return refined


def vmem():
    return pl.BlockSpec(memory_space=pltpu.VMEM)


def hbm():
    return pl.BlockSpec(memory_space=pltpu.HBM)


def unread():
    return pl.BlockSpec(memory_space=pl.ANY)


def like(x):
    return jax.ShapeDtypeStruct(x.shape, x.dtype)


def join_kernel(after_n, *refs):
    gather_rows(refs[after_n:-1], refs[-1])


def join(parts, *after):
    rows = sum(part.shape[0] for part in parts)
    return pl.pallas_call(
        functools.partial(join_kernel, len(after)),
        out_shape=jax.ShapeDtypeStruct((rows, parts[0].shape[1]), parts[0].dtype),
        in_specs=[unread()] * len(after) + [vmem()] * len(parts),
        out_specs=vmem(),
        compiler_params=pltpu.CompilerParams(vmem_limit_bytes=vmem_limit),
        cost_estimate=cost(),
        name="join",
    )(*after, *parts)


def pack_kernel(dest_from, points, *refs):
    packed, (dest, rows, dest_arrival, arrival) = refs[:-4], refs[-4:]
    dest_copy = pltpu.make_async_copy(dest_from, dest, dest_arrival)
    dest_copy.start()
    copy = pltpu.make_async_copy(points, rows, arrival)
    copy.start()
    count = len(packed)
    row_count = rows.shape[0]
    capacity = row_count // count
    dest_copy.wait()
    apart = jnp.bitwise_xor(dest[...], lax.axis_index("group"))
    named = lax.broadcasted_iota(jnp.int32, (8, row_count), 0) == apart
    row_at = lax.broadcasted_iota(jnp.int32, (row_count, row_count), 0)
    col_at = lax.broadcasted_iota(jnp.int32, (row_count, row_count), 1)
    before = (row_at < col_at).astype(jnp.bfloat16)
    named = named.astype(jnp.float32)
    earlier = jnp.dot(named.astype(jnp.bfloat16), before, preferred_element_type=jnp.float32)
    rank = jnp.sum(earlier * named, axis=0, keepdims=True)
    slot = apart * capacity + rank.astype(jnp.int32)
    placement = (row_at == slot).astype(jnp.bfloat16)
    copy.wait()
    for k in range(count):
        part = placement[k * capacity : (k + 1) * capacity]
        packed[k][...] = jnp.dot(part, rows[...], preferred_element_type=jnp.float32).astype(
            jnp.bfloat16
        )


def pack(dest_row, points, group_count):
    row_count, feature_dim = points.shape
    capacity = row_count // group_count
    return pl.pallas_call(
        pack_kernel,
        out_shape=[jax.ShapeDtypeStruct((capacity, feature_dim), points.dtype)] * group_count,
        in_specs=[hbm(), hbm()],
        out_specs=[vmem()] * group_count,
        scratch_shapes=[
            pltpu.VMEM((1, row_count), jnp.int32),
            pltpu.VMEM((row_count, feature_dim), points.dtype),
            pltpu.SemaphoreType.DMA,
            pltpu.SemaphoreType.DMA,
        ],
        compiler_params=pltpu.CompilerParams(vmem_limit_bytes=vmem_limit),
        cost_estimate=cost(),
        name="pack",
    )(dest_row, points)


def scaled_scores(table, half_norms, rows):
    dims = (((1,), (1,)), ((), ()))
    product = lax.dot_general(table, rows, dims, preferred_element_type=jnp.float32)
    return exponent_scale * (product - half_norms)


def softmax_terms(table, half_norms, rows, scores, tile):
    row_count = rows.shape[0]
    top = jnp.full((1, row_count), -jnp.inf, jnp.float32)
    total = jnp.zeros((1, row_count), jnp.float32)
    for start in range(0, table.shape[0], tile):
        at = slice(start, start + tile)
        block = scaled_scores(table[at, :], half_norms[at, :], rows)
        scores[at, :] = block
        higher = jnp.maximum(top, jnp.max(block, axis=0, keepdims=True))
        here = jnp.sum(jnp.exp2(block - higher), axis=0, keepdims=True)
        total = total * jnp.exp2(top - higher) + here
        top = higher
    return top, 1.0 / total


def gather_rows(parts, rows):
    start = 0
    for part in parts:
        rows[start : start + part.shape[0], :] = part[...]
        start += part.shape[0]


def tile_sums(scores, top, inverse, rows):
    weights = (jnp.exp2(scores - top) * inverse).astype(jnp.bfloat16)
    sums = jnp.dot(weights, rows, preferred_element_type=jnp.float32)
    count = jnp.sum(weights.astype(jnp.float32), axis=1, keepdims=True)
    return sums, jnp.broadcast_to(count, (count.shape[0], lanes))


def at_tile(index, tile):
    return pl.ds(pl.multiple_of(index * tile, tile), tile)


def chip_place():
    member = lax.axis_index("member")
    core = member % 2
    return member // 2, core, member, member + 1 - 2 * core


def two_tiles(table, half_norms, rows, scores, before, after, tile):
    feature_dim = rows.shape[1]
    _, _, mine, other = chip_place()
    terms = softmax_terms(table, half_norms, rows, scores, tile)
    for index, so_far, out in zip((mine, other), before, after):
        sums, count = tile_sums(scores[at_tile(index, tile), :], *terms, rows)
        if so_far is not None:
            sums = sums + so_far[:, :feature_dim]
            count = count + so_far[:, feature_dim:]
        out[:, :feature_dim] = sums
        out[:, feature_dim:] = count


def own_kernel(tile, table, rows, keep, give, half_norms, scores):
    for start in range(0, table.shape[0], tile):
        block = table[start : start + tile, :].astype(jnp.float32)
        half_norms[start : start + tile, :] = 0.5 * jnp.sum(block * block, axis=1, keepdims=True)
    two_tiles(table, half_norms, rows[...], scores, (None, None), (keep, give), tile)


def step_kernel(tile, step, depth, table, half_norms, keep_in, give_in, rows, keep, give, scores):
    level, core, _, _ = chip_place()
    here = ((core == 0) & (level >= step)) | ((core == 1) & (level < depth - step))

    @pl.when(jnp.logical_not(here))
    def _():
        keep[...] = keep_in[...]
        give[...] = give_in[...]

    @pl.when(here)
    def _():
        two_tiles(table, half_norms, rows[...], scores, (keep_in, give_in), (keep, give), tile)


def last_sums(tile, depth, table, half_norms, came, passed, rows, scores):
    level, core, mine, _ = chip_place()
    here = ((core == 0) & (level == depth - 1)) | ((core == 1) & (level == 0))

    @pl.when(here)
    def _():
        rows[...] = came[...]

    @pl.when(jnp.logical_not(here))
    def _():
        rows[...] = passed[...]

    all_rows = rows[...]
    terms = softmax_terms(table, half_norms, all_rows, scores, tile)
    return tile_sums(scores[at_tile(mine, tile), :], *terms, all_rows)


def end_chip(depth):
    level = chip_place()[0]
    return (level == 0) | (level == depth - 1)


def end_kernel(tile, depth, table, half_norms, keep_in, came, passed, keep, rows, scores):
    feature_dim = rows.shape[1]

    @pl.when(jnp.logical_not(end_chip(depth)))
    def _():
        keep[...] = keep_in[...]

    @pl.when(end_chip(depth))
    def _():
        sums, count = last_sums(tile, depth, table, half_norms, came, passed, rows, scores)
        keep[:, :feature_dim] = keep_in[:, :feature_dim] + sums
        keep[:, feature_dim:] = keep_in[:, feature_dim:] + count


def refit_kernel(tile, depth, table, half_norms, keep, got, came, passed, refined, rows, scores):
    feature_dim = rows.shape[1]
    mine = chip_place()[2]
    old = table[at_tile(mine, tile), :].astype(jnp.float32)

    def refit(more, count):
        sums = keep[:, :feature_dim] + got[:, :feature_dim] + more
        count = keep[:, feature_dim:] + got[:, feature_dim:] + count
        scale = 1.0 / (count[:, :1] + 1.0)
        refined[...] = ((sums + old) * scale).astype(jnp.bfloat16)

    @pl.when(jnp.logical_not(end_chip(depth)))
    def _():
        refit(0.0, 0.0)

    @pl.when(end_chip(depth))
    def _():
        refit(*last_sums(tile, depth, table, half_norms, came, passed, rows, scores))


def cost():
    return pl.CostEstimate(flops=1 << 20, bytes_accessed=0, transcendentals=0)


def handoff(points, centroids, dest_group):
    group_count = lax.axis_size("group")
    member_count = lax.axis_size("member")
    depth = member_count // 2
    row_count, feature_dim = points.shape
    fine_count = centroids.shape[0]
    tile = fine_count // member_count

    def swap(x):
        return lax.ppermute(x, "member", [(i, i ^ 1) for i in range(member_count)])

    def onward(x, step):
        up = [(2 * z, 2 * z + 2) for z in range(step - 1, depth - 1)]
        down = [(2 * z + 3, 2 * z + 1) for z in range(0, depth - step)]
        return lax.ppermute(x, "member", up + down)

    sums_shape = jax.ShapeDtypeStruct((tile, feature_dim + lanes), jnp.float32)
    norms_shape = jax.ShapeDtypeStruct((fine_count, 1), jnp.float32)

    def kernel(body, out_shape, *operands, scratch_rows=0, aliases={}):
        scratch = [pltpu.VMEM((fine_count, row_count), jnp.float32)]
        if scratch_rows:
            scratch = [pltpu.VMEM((scratch_rows, feature_dim), jnp.bfloat16)] + scratch
        return pl.pallas_call(
            body,
            out_shape=out_shape,
            in_specs=[vmem()] * len(operands),
            out_specs=jax.tree.map(lambda _: vmem(), out_shape),
            scratch_shapes=scratch,
            input_output_aliases=aliases,
            compiler_params=pltpu.CompilerParams(vmem_limit_bytes=vmem_limit),
            cost_estimate=cost(),
            name=body.func.__name__,
        )(*operands)

    packed = pack(dest_group.reshape(1, row_count), points, group_count)
    fetched = [
        lax.ppermute(packed[k], "group", [(i, i ^ k) for i in range(group_count)])
        for k in reversed(range(1, group_count))
    ]
    own = join([packed[0]] + fetched)
    first, second = onward(own, 1), onward(swap(own), 1)
    keep, give, half_norms = kernel(
        functools.partial(own_kernel, tile), [sums_shape, sums_shape, norms_shape], centroids, own
    )
    for step in range(1, depth - 1):
        held = join([first], keep)
        next_first = onward(held, step + 1)
        body = functools.partial(step_kernel, tile, step, depth)
        keep, give = kernel(
            body, [sums_shape] * 2, centroids, half_norms, keep, give, held, aliases={2: 0, 3: 1}
        )
        held = join([second], keep)
        next_second = onward(held, step + 1)
        keep, give = kernel(
            body, [sums_shape] * 2, centroids, half_norms, keep, give, held, aliases={2: 0, 3: 1}
        )
        first, second = next_first, next_second

    got = swap(give)
    held = join([first], keep)
    keep = kernel(
        functools.partial(end_kernel, tile, depth), sums_shape, centroids, half_norms, keep, held,
        swap(held), scratch_rows=row_count, aliases={2: 0},
    )
    held = join([second], keep)
    return kernel(
        functools.partial(refit_kernel, tile, depth),
        jax.ShapeDtypeStruct((tile, feature_dim), jnp.bfloat16),
        centroids, half_norms, keep, got, held, swap(held), scratch_rows=row_count,
    )


def solution(mesh):
    def local(points, centroids, dest_group):
        groups, members = mesh.shape["group"], mesh.shape["member"]
        if groups * (points.shape[0] // 4) == points.shape[0] and 6 <= members <= 16:
            return handoff(points, centroids, dest_group)
        return general(points, centroids, dest_group)

    return jax.shard_map(
        local,
        mesh=mesh,
        in_specs=(P(("group", "member"), None), P("group", None), P(("group", "member"), None)),
        out_specs=P(("group", "member"), None),
        check_vma=False,
    )
```

```python
import functools
import math

import jax
import jax.numpy as jnp
from jax import lax
from jax.experimental import pallas as pl
from jax.experimental.pallas import tpu as pltpu
from jax.sharding import PartitionSpec as P

score_scale = 0.15
lanes = 128
exponent_scale = score_scale * math.log2(math.e)
vmem_limit = 20 * 1024 * 1024


def general(points, centroids, dest_group):
    group_count = lax.axis_size("group")
    member_count = lax.axis_size("member")
    point_rows = points.shape[0]
    capacity = point_rows // 4
    feature_dim = points.shape[1]
    fine_count = centroids.shape[0]
    destination = dest_group[:, 0]
    in_group = (destination[:, None] == jnp.arange(group_count, dtype=jnp.int32)[None, :]).astype(
        jnp.int32
    )
    earlier = jnp.cumsum(in_group, axis=0) - in_group
    own_rank = jnp.sum(earlier * in_group, axis=1)
    slot_index = destination * capacity + own_rank
    placement = (
        jnp.arange(group_count * capacity, dtype=jnp.int32)[:, None] == slot_index[None, :]
    ).astype(jnp.bfloat16)
    packed = jnp.dot(placement, points, preferred_element_type=jnp.float32).astype(jnp.bfloat16)
    packed = packed.reshape(group_count, capacity, feature_dim)
    slot_flags = jnp.dot(
        placement, jnp.ones((point_rows, 1), jnp.bfloat16), preferred_element_type=jnp.float32
    )
    slot_flags = slot_flags.astype(jnp.bfloat16).reshape(group_count, capacity, 1)
    centroid_f = centroids.astype(jnp.float32)
    centroid_norms = jnp.sum(centroid_f * centroid_f, axis=1)
    arrived, marks = (
        lax.all_to_all(packed, "group", split_axis=0, concat_axis=0, tiled=True),
        lax.all_to_all(slot_flags, "group", split_axis=0, concat_axis=0, tiled=True),
    )
    rows = arrived.reshape(-1, feature_dim)
    scores = score_scale * (
        jnp.dot(rows, centroids.T, preferred_element_type=jnp.float32)
        - 0.5 * centroid_norms[None, :]
    )
    weights = jax.nn.softmax(scores, axis=-1) * marks.reshape(-1, 1).astype(jnp.float32)
    responsibility = weights.astype(jnp.bfloat16).reshape(
        arrived.shape[0], arrived.shape[1], fine_count
    )
    all_rows = arrived.reshape(-1, feature_dim)
    all_weights = responsibility.reshape(-1, fine_count)
    weighted = jnp.dot(all_weights.T, all_rows, preferred_element_type=jnp.float32)
    soft_counts = jnp.dot(
        jnp.ones((1, all_weights.shape[0]), jnp.bfloat16),
        all_weights,
        preferred_element_type=jnp.float32,
    )[0]
    member_index = lax.axis_index("member")
    tile_sums, tile_counts = (
        lax.psum_scatter(weighted, "member", scatter_dimension=0, tiled=True),
        lax.psum_scatter(soft_counts, "member", scatter_dimension=0, tiled=True),
    )
    tile_rows = fine_count // member_count
    old_tile = lax.dynamic_slice_in_dim(centroid_f, member_index * tile_rows, tile_rows, 0)
    refined = ((tile_sums + old_tile) / (tile_counts + 1.0)[:, None]).astype(jnp.bfloat16)
    return refined


def vmem():
    return pl.BlockSpec(memory_space=pltpu.VMEM)


def hbm():
    return pl.BlockSpec(memory_space=pltpu.HBM)


def unread():
    return pl.BlockSpec(memory_space=pl.ANY)


def like(x):
    return jax.ShapeDtypeStruct(x.shape, x.dtype)


def join_kernel(after_n, *refs):
    gather_rows(refs[after_n:-1], refs[-1])


def join(parts, *after):
    rows = sum(part.shape[0] for part in parts)
    return pl.pallas_call(
        functools.partial(join_kernel, len(after)),
        out_shape=jax.ShapeDtypeStruct((rows, parts[0].shape[1]), parts[0].dtype),
        in_specs=[unread()] * len(after) + [vmem()] * len(parts),
        out_specs=vmem(),
        compiler_params=pltpu.CompilerParams(vmem_limit_bytes=vmem_limit),
        cost_estimate=cost(),
        name="join",
    )(*after, *parts)


def pick_kernel(depth, own, came, after, out):
    level, core, _, _ = chip_place()
    forwards = ((core == 0) & (level == depth - 2)) | ((core == 1) & (level == 1))

    @pl.when(forwards)
    def _():
        out[...] = came[...]

    @pl.when(jnp.logical_not(forwards))
    def _():
        out[...] = own[...]


def pick(depth, own, came, after):
    return pl.pallas_call(
        functools.partial(pick_kernel, depth),
        out_shape=like(own),
        in_specs=[vmem(), vmem(), unread()],
        out_specs=vmem(),
        compiler_params=pltpu.CompilerParams(vmem_limit_bytes=vmem_limit),
        cost_estimate=cost(),
        name="pick",
    )(own, came, after)


def pack_kernel(dest_from, points, *refs):
    packed, (dest, rows, dest_arrival, arrival) = refs[:-4], refs[-4:]
    dest_copy = pltpu.make_async_copy(dest_from, dest, dest_arrival)
    dest_copy.start()
    copy = pltpu.make_async_copy(points, rows, arrival)
    copy.start()
    count = len(packed)
    row_count = rows.shape[0]
    capacity = row_count // count
    dest_copy.wait()
    apart = jnp.bitwise_xor(dest[...], lax.axis_index("group"))
    named = lax.broadcasted_iota(jnp.int32, (8, row_count), 0) == apart
    row_at = lax.broadcasted_iota(jnp.int32, (row_count, row_count), 0)
    col_at = lax.broadcasted_iota(jnp.int32, (row_count, row_count), 1)
    before = (row_at < col_at).astype(jnp.bfloat16)
    named = named.astype(jnp.float32)
    earlier = jnp.dot(named.astype(jnp.bfloat16), before, preferred_element_type=jnp.float32)
    rank = jnp.sum(earlier * named, axis=0, keepdims=True)
    slot = apart * capacity + rank.astype(jnp.int32)
    placement = (row_at == slot).astype(jnp.bfloat16)
    copy.wait()
    for k in range(count):
        part = placement[k * capacity : (k + 1) * capacity]
        packed[k][...] = jnp.dot(part, rows[...], preferred_element_type=jnp.float32).astype(
            jnp.bfloat16
        )


def pack(dest_row, points, group_count):
    row_count, feature_dim = points.shape
    capacity = row_count // group_count
    return pl.pallas_call(
        pack_kernel,
        out_shape=[jax.ShapeDtypeStruct((capacity, feature_dim), points.dtype)] * group_count,
        in_specs=[hbm(), hbm()],
        out_specs=[vmem()] * group_count,
        scratch_shapes=[
            pltpu.VMEM((1, row_count), jnp.int32),
            pltpu.VMEM((row_count, feature_dim), points.dtype),
            pltpu.SemaphoreType.DMA,
            pltpu.SemaphoreType.DMA,
        ],
        compiler_params=pltpu.CompilerParams(vmem_limit_bytes=vmem_limit),
        cost_estimate=cost(),
        name="pack",
    )(dest_row, points)


def scaled_scores(table, half_norms, rows):
    dims = (((1,), (1,)), ((), ()))
    product = lax.dot_general(table, rows, dims, preferred_element_type=jnp.float32)
    return exponent_scale * (product - half_norms)


def softmax_terms(table, half_norms, rows, scores, tile):
    row_count = rows.shape[0]
    top = jnp.full((1, row_count), -jnp.inf, jnp.float32)
    total = jnp.zeros((1, row_count), jnp.float32)
    for start in range(0, table.shape[0], tile):
        at = slice(start, start + tile)
        block = scaled_scores(table[at, :], half_norms[at, :], rows)
        scores[at, :] = block
        higher = jnp.maximum(top, jnp.max(block, axis=0, keepdims=True))
        here = jnp.sum(jnp.exp2(block - higher), axis=0, keepdims=True)
        total = total * jnp.exp2(top - higher) + here
        top = higher
    return top, 1.0 / total


def gather_rows(parts, rows):
    start = 0
    for part in parts:
        if part is rows:
            return
        rows[start : start + part.shape[0], :] = part[...]
        start += part.shape[0]


def tile_sums(scores, top, inverse, rows):
    weights = (jnp.exp2(scores - top) * inverse).astype(jnp.bfloat16)
    sums = jnp.dot(weights, rows, preferred_element_type=jnp.float32)
    count = jnp.sum(weights.astype(jnp.float32), axis=1, keepdims=True)
    return sums, jnp.broadcast_to(count, (count.shape[0], lanes))


def at_tile(index, tile):
    return pl.ds(pl.multiple_of(index * tile, tile), tile)


def chip_place():
    member = lax.axis_index("member")
    core = member % 2
    return member // 2, core, member, member + 1 - 2 * core


def add_rows(table, half_norms, parts, rows, scores, sums, tile):
    feature_dim = table.shape[1]
    gather_rows(parts, rows)
    count = sum(part.shape[0] for part in parts)
    all_rows = rows[:count, :]
    scores = scores.at[:, :count]
    terms = softmax_terms(table, half_norms, all_rows, scores, tile)
    for index, out in sums:
        more, count = tile_sums(scores[at_tile(index, tile), :], *terms, all_rows)
        out[:, :feature_dim] += more
        out[:, feature_dim:] += count


def own_kernel(tile, table, own, keep, give, half_norms, rows, scores):
    for start in range(0, table.shape[0], tile):
        block = table[start : start + tile, :].astype(jnp.float32)
        half_norms[start : start + tile, :] = 0.5 * jnp.sum(block * block, axis=1, keepdims=True)
    _, _, mine, other = chip_place()
    keep[...] = jnp.zeros_like(keep)
    give[...] = jnp.zeros_like(give)
    add_rows(table, half_norms, [own], rows, scores, ((mine, keep), (other, give)), tile)


def came_to(step, depth):
    level, core, _, _ = chip_place()
    return ((core == 0) & (level >= step)) | ((core == 1) & (level < depth - step))


def step_kernel(tile, depth, step, table, half_norms, keep_in, give_in, *refs):
    parts, (keep, give, rows, scores) = refs[:-4], refs[-4:]
    keep[...] = keep_in[...]
    give[...] = give_in[...]

    @pl.when(came_to(step, depth))
    def _():
        _, _, mine, other = chip_place()
        add_rows(table, half_norms, parts, rows, scores, ((mine, keep), (other, give)), tile)


def end_chip(depth):
    level = chip_place()[0]
    return (level == 0) | (level == depth - 1)


def add_last(tile, depth, table, half_norms, parts, keep, rows, scores):
    half = len(parts) // 2
    mine = chip_place()[2]

    @pl.when(came_to(depth - 1, depth))
    def _():
        gather_rows(parts[:half], rows)

    @pl.when(jnp.logical_not(came_to(depth - 1, depth)))
    def _():
        gather_rows(parts[half:], rows)

    add_rows(table, half_norms, [rows], rows, scores, ((mine, keep),), tile)


def refit_kernel(tile, depth, table, half_norms, keep, got, *refs):
    parts, (refined, rows, scores, sums) = refs[:-4], refs[-4:]
    feature_dim = table.shape[1]
    mine = chip_place()[2]
    sums[...] = keep[...] + got[...]

    @pl.when(end_chip(depth))
    def _():
        add_last(tile, depth, table, half_norms, parts, sums, rows, scores)

    old = table[at_tile(mine, tile), :].astype(jnp.float32)
    scale = 1.0 / (sums[:, feature_dim : feature_dim + 1] + 1.0)
    refined[...] = ((sums[:, :feature_dim] + old) * scale).astype(jnp.bfloat16)


def cost(flops=1 << 20):
    return pl.CostEstimate(flops=flops, bytes_accessed=0, transcendentals=0)


def handoff(points, centroids, dest_group):
    group_count = lax.axis_size("group")
    member_count = lax.axis_size("member")
    depth = member_count // 2
    row_count, feature_dim = points.shape
    fine_count = centroids.shape[0]
    tile = fine_count // member_count

    def swap(x):
        return lax.ppermute(x, "member", [(i, i ^ 1) for i in range(member_count)])

    def along(x, moves):
        up = [(2 * z, 2 * to) for z, to in moves]
        down = [(2 * (depth - 1 - z) + 1, 2 * (depth - 1 - to) + 1) for z, to in moves]
        return lax.ppermute(x, "member", up + down)

    last = depth - 1
    apart = [(0, last - 1), (last - 1, last)]
    over = [(1, last)]
    beside = [(z, z + 1) for z in range(last)]

    sums_shape = jax.ShapeDtypeStruct((tile, feature_dim + lanes), jnp.float32)
    norms_shape = jax.ShapeDtypeStruct((fine_count, 1), jnp.float32)

    def kernel(body, out_shape, *operands, scratch=(), aliases={}, flops=1 << 20):
        return pl.pallas_call(
            body,
            out_shape=out_shape,
            in_specs=[vmem()] * len(operands),
            out_specs=jax.tree.map(lambda _: vmem(), out_shape),
            scratch_shapes=scratch,
            input_output_aliases=aliases,
            compiler_params=pltpu.CompilerParams(vmem_limit_bytes=vmem_limit),
            cost_estimate=cost(flops),
            name=body.func.__name__,
        )(*operands)

    def scratch(rows):
        return [
            pltpu.VMEM((rows, feature_dim), jnp.bfloat16),
            pltpu.VMEM((fine_count, rows), jnp.float32),
        ]

    packed = pack(dest_group.reshape(1, row_count), points, group_count)
    fetched = [
        lax.ppermute(packed[k], "group", [(i, i ^ k) for i in range(group_count)])
        for k in reversed(range(1, group_count))
    ]
    first = join([packed[0]] + fetched)
    over_first = along(first, over)
    apart_first = along(first, apart)
    second = swap(first)
    apart_second = along(second, apart)
    two_sums = [sums_shape, sums_shape]
    keep, give, half_norms = kernel(
        functools.partial(own_kernel, tile),
        [*two_sums, norms_shape],
        centroids,
        first,
        scratch=scratch(row_count),
    )

    def add(step, keep, give, *parts):
        return kernel(
            functools.partial(step_kernel, tile, depth, step),
            two_sums,
            centroids,
            half_norms,
            keep,
            give,
            *parts,
            scratch=scratch(len(parts) * row_count),
            aliases={2: 0, 3: 1},
            flops=1 << 28,
        )

    beside_first = along(pick(depth, first, apart_first, keep), beside)
    beside_second = along(pick(depth, second, apart_second, keep), beside)
    over_second = along(second, over)
    keep, give = add(last - 1, keep, give, apart_first, apart_second)
    keep, give = add(last, keep, give, over_first)
    keep, give = add(1, keep, give, beside_first, beside_second)
    got = jnp.concatenate([swap(give[: tile // 2]), swap(give[tile // 2 :])], axis=0)
    held = join([over_second], keep)
    return kernel(
        functools.partial(refit_kernel, tile, depth),
        jax.ShapeDtypeStruct((tile, feature_dim), jnp.bfloat16),
        centroids,
        half_norms,
        keep,
        got,
        held,
        swap(held),
        scratch=scratch(row_count) + [pltpu.VMEM(sums_shape.shape, jnp.float32)],
    )


def solution(mesh):
    def local(points, centroids, dest_group):
        groups, members = mesh.shape["group"], mesh.shape["member"]
        if groups * (points.shape[0] // 4) == points.shape[0] and members // 2 == 4:
            return handoff(points, centroids, dest_group)
        return general(points, centroids, dest_group)

    return jax.shard_map(
        local,
        mesh=mesh,
        in_specs=(P(("group", "member"), None), P("group", None), P(("group", "member"), None)),
        out_specs=P(("group", "member"), None),
        check_vma=False,
    )
```

```python
import functools
import math

import jax
import jax.numpy as jnp
from jax import lax
from jax.experimental import pallas as pl
from jax.experimental.pallas import tpu as pltpu
from jax.sharding import PartitionSpec as P

score_scale = 0.15
lanes = 128
exponent_scale = score_scale * math.log2(math.e)
own_flops = 1 << 31
beside_flops = 1 << 28
over_flops = 1 << 32
last_flops = 1 << 26
vmem_limit = 20 * 1024 * 1024


def general(points, centroids, dest_group):
    group_count = lax.axis_size("group")
    member_count = lax.axis_size("member")
    point_rows = points.shape[0]
    capacity = point_rows // 4
    feature_dim = points.shape[1]
    fine_count = centroids.shape[0]
    destination = dest_group[:, 0]
    in_group = (destination[:, None] == jnp.arange(group_count, dtype=jnp.int32)[None, :]).astype(
        jnp.int32
    )
    earlier = jnp.cumsum(in_group, axis=0) - in_group
    own_rank = jnp.sum(earlier * in_group, axis=1)
    slot_index = destination * capacity + own_rank
    placement = (
        jnp.arange(group_count * capacity, dtype=jnp.int32)[:, None] == slot_index[None, :]
    ).astype(jnp.bfloat16)
    packed = jnp.dot(placement, points, preferred_element_type=jnp.float32).astype(jnp.bfloat16)
    packed = packed.reshape(group_count, capacity, feature_dim)
    slot_flags = jnp.dot(
        placement, jnp.ones((point_rows, 1), jnp.bfloat16), preferred_element_type=jnp.float32
    )
    slot_flags = slot_flags.astype(jnp.bfloat16).reshape(group_count, capacity, 1)
    centroid_f = centroids.astype(jnp.float32)
    centroid_norms = jnp.sum(centroid_f * centroid_f, axis=1)
    arrived, marks = (
        lax.all_to_all(packed, "group", split_axis=0, concat_axis=0, tiled=True),
        lax.all_to_all(slot_flags, "group", split_axis=0, concat_axis=0, tiled=True),
    )
    rows = arrived.reshape(-1, feature_dim)
    scores = score_scale * (
        jnp.dot(rows, centroids.T, preferred_element_type=jnp.float32)
        - 0.5 * centroid_norms[None, :]
    )
    weights = jax.nn.softmax(scores, axis=-1) * marks.reshape(-1, 1).astype(jnp.float32)
    responsibility = weights.astype(jnp.bfloat16).reshape(
        arrived.shape[0], arrived.shape[1], fine_count
    )
    all_rows = arrived.reshape(-1, feature_dim)
    all_weights = responsibility.reshape(-1, fine_count)
    weighted = jnp.dot(all_weights.T, all_rows, preferred_element_type=jnp.float32)
    soft_counts = jnp.dot(
        jnp.ones((1, all_weights.shape[0]), jnp.bfloat16),
        all_weights,
        preferred_element_type=jnp.float32,
    )[0]
    member_index = lax.axis_index("member")
    tile_sums, tile_counts = (
        lax.psum_scatter(weighted, "member", scatter_dimension=0, tiled=True),
        lax.psum_scatter(soft_counts, "member", scatter_dimension=0, tiled=True),
    )
    tile_rows = fine_count // member_count
    old_tile = lax.dynamic_slice_in_dim(centroid_f, member_index * tile_rows, tile_rows, 0)
    refined = ((tile_sums + old_tile) / (tile_counts + 1.0)[:, None]).astype(jnp.bfloat16)
    return refined


def vmem():
    return pl.BlockSpec(memory_space=pltpu.VMEM)


def hbm():
    return pl.BlockSpec(memory_space=pltpu.HBM)


def unread():
    return pl.BlockSpec(memory_space=pl.ANY)


def like(x):
    return jax.ShapeDtypeStruct(x.shape, x.dtype)


def join_kernel(after_n, *refs):
    gather_rows(refs[after_n:-1], refs[-1])


def join(parts, *after, flops=1 << 20):
    rows = sum(part.shape[0] for part in parts)
    return pl.pallas_call(
        functools.partial(join_kernel, len(after)),
        out_shape=jax.ShapeDtypeStruct((rows, parts[0].shape[1]), parts[0].dtype),
        in_specs=[unread()] * len(after) + [vmem()] * len(parts),
        out_specs=vmem(),
        compiler_params=pltpu.CompilerParams(vmem_limit_bytes=vmem_limit),
        cost_estimate=cost(flops),
        name="join",
    )(*after, *parts)


def pick_kernel(depth, own, came, after, out):
    level, core, _, _ = chip_place()
    forwards = ((core == 0) & (level == depth - 2)) | ((core == 1) & (level == 1))

    @pl.when(forwards)
    def _():
        out[...] = came[...]

    @pl.when(jnp.logical_not(forwards))
    def _():
        out[...] = own[...]


def pick(depth, own, came, after):
    return pl.pallas_call(
        functools.partial(pick_kernel, depth),
        out_shape=like(own),
        in_specs=[vmem(), vmem(), unread()],
        out_specs=vmem(),
        compiler_params=pltpu.CompilerParams(vmem_limit_bytes=vmem_limit),
        cost_estimate=cost(),
        name="pick",
    )(own, came, after)


def pack_kernel(dest_from, points, *refs):
    packed, (dest, rows, dest_arrival, arrival) = refs[:-4], refs[-4:]
    dest_copy = pltpu.make_async_copy(dest_from, dest, dest_arrival)
    dest_copy.start()
    copy = pltpu.make_async_copy(points, rows, arrival)
    copy.start()
    count = len(packed)
    row_count = rows.shape[0]
    capacity = row_count // count
    dest_copy.wait()
    apart = jnp.bitwise_xor(dest[...], lax.axis_index("group"))
    named = lax.broadcasted_iota(jnp.int32, (8, row_count), 0) == apart
    row_at = lax.broadcasted_iota(jnp.int32, (row_count, row_count), 0)
    col_at = lax.broadcasted_iota(jnp.int32, (row_count, row_count), 1)
    before = (row_at < col_at).astype(jnp.bfloat16)
    named = named.astype(jnp.float32)
    earlier = jnp.dot(named.astype(jnp.bfloat16), before, preferred_element_type=jnp.float32)
    rank = jnp.sum(earlier * named, axis=0, keepdims=True)
    slot = apart * capacity + rank.astype(jnp.int32)
    placement = (row_at == slot).astype(jnp.bfloat16)
    copy.wait()
    for k in range(count):
        part = placement[k * capacity : (k + 1) * capacity]
        packed[k][...] = jnp.dot(part, rows[...], preferred_element_type=jnp.float32).astype(
            jnp.bfloat16
        )


def pack(dest_row, points, group_count):
    row_count, feature_dim = points.shape
    capacity = row_count // group_count
    return pl.pallas_call(
        pack_kernel,
        out_shape=[jax.ShapeDtypeStruct((capacity, feature_dim), points.dtype)] * group_count,
        in_specs=[hbm(), hbm()],
        out_specs=[vmem()] * group_count,
        scratch_shapes=[
            pltpu.VMEM((1, row_count), jnp.int32),
            pltpu.VMEM((row_count, feature_dim), points.dtype),
            pltpu.SemaphoreType.DMA,
            pltpu.SemaphoreType.DMA,
        ],
        compiler_params=pltpu.CompilerParams(vmem_limit_bytes=vmem_limit),
        cost_estimate=cost(),
        name="pack",
    )(
        pltpu.with_memory_space_constraint(dest_row, pltpu.HBM),
        pltpu.with_memory_space_constraint(points, pltpu.HBM),
    )


def scaled_scores(table, half_norms, rows):
    dims = (((1,), (1,)), ((), ()))
    product = lax.dot_general(table, rows, dims, preferred_element_type=jnp.float32)
    return exponent_scale * (product - half_norms)


def softmax_terms(table, half_norms, rows, scores, tile):
    row_count = rows.shape[0]
    top = jnp.full((1, row_count), -jnp.inf, jnp.float32)
    total = jnp.zeros((1, row_count), jnp.float32)
    for start in range(0, table.shape[0], tile):
        at = slice(start, start + tile)
        block = scaled_scores(table[at, :], half_norms[at, :], rows)
        scores[at, :] = block
        higher = jnp.maximum(top, jnp.max(block, axis=0, keepdims=True))
        here = jnp.sum(jnp.exp2(block - higher), axis=0, keepdims=True)
        total = total * jnp.exp2(top - higher) + here
        top = higher
    return top, 1.0 / total


def gather_rows(parts, rows):
    start = 0
    for part in parts:
        if part is rows:
            return
        rows[start : start + part.shape[0], :] = part[...]
        start += part.shape[0]


def tile_sums(scores, top, inverse, rows):
    weights = (jnp.exp2(scores - top) * inverse).astype(jnp.bfloat16)
    sums = jnp.dot(weights, rows, preferred_element_type=jnp.float32)
    count = jnp.sum(weights.astype(jnp.float32), axis=1, keepdims=True)
    return sums, jnp.broadcast_to(count, (count.shape[0], lanes))


def at_tile(index, tile):
    return pl.ds(pl.multiple_of(index * tile, tile), tile)


def chip_place():
    member = lax.axis_index("member")
    core = member % 2
    return member // 2, core, member, member + 1 - 2 * core


def add_rows(table, half_norms, parts, rows, scores, sums, tile):
    feature_dim = table.shape[1]
    gather_rows(parts, rows)
    count = sum(part.shape[0] for part in parts)
    all_rows = rows[:count, :]
    scores = scores.at[:, :count]
    terms = softmax_terms(table, half_norms, all_rows, scores, tile)
    for index, out in sums:
        more, count = tile_sums(scores[at_tile(index, tile), :], *terms, all_rows)
        out[:, :feature_dim] += more
        out[:, feature_dim:] += count


def came_to(step, depth):
    level, core, _, _ = chip_place()
    return ((core == 0) & (level >= step)) | ((core == 1) & (level < depth - step))


def first_kernel(tile, depth, table_from, near, far, apart, over, *refs):
    table, keep, give, half_norms, arrivals, rows, scores = refs
    copies = []
    for index in range(arrivals.shape[0]):
        at = pl.ds(index * tile, tile)
        copies.append(pltpu.make_async_copy(table_from.at[at], table.at[at], arrivals.at[index]))
    for copy in copies:
        copy.start()
    keep[...] = jnp.zeros_like(keep)
    give[...] = jnp.zeros_like(give)
    for index, copy in enumerate(copies):
        copy.wait()
        at = slice(index * tile, (index + 1) * tile)
        block = table[at, :].astype(jnp.float32)
        half_norms[at, :] = 0.5 * jnp.sum(block * block, axis=1, keepdims=True)

    @pl.when(came_to(depth - 1, depth))
    def _():
        _, _, mine, other = chip_place()
        parts = (near, far, apart, over)
        add_rows(table, half_norms, parts, rows, scores, ((mine, keep), (other, give)), tile)


def own_kernel(tile, depth, table, half_norms, keep_in, give_in, near, far, apart_near, *refs):
    came, (keep, give, rows, scores) = refs[:-4], refs[-4:]
    keep[...] = keep_in[...]
    give[...] = give_in[...]
    _, _, mine, other = chip_place()

    def add(*parts):
        add_rows(table, half_norms, parts, rows, scores, ((mine, keep), (other, give)), tile)

    end, here = came_to(depth - 1, depth), came_to(depth - 2, depth)

    @pl.when(end)
    def _():
        add(*came)

    @pl.when(here & jnp.logical_not(end))
    def _():
        add(near, far, apart_near, *came)

    @pl.when(jnp.logical_not(here))
    def _():
        add(near, far)


def step_kernel(tile, depth, step, table, half_norms, keep_in, give_in, *refs):
    parts, (keep, give, rows, scores) = refs[:-4], refs[-4:]
    keep[...] = keep_in[...]
    give[...] = give_in[...]

    @pl.when(came_to(step, depth))
    def _():
        _, _, mine, other = chip_place()
        add_rows(table, half_norms, parts, rows, scores, ((mine, keep), (other, give)), tile)


def end_chip(depth):
    level = chip_place()[0]
    return (level == 0) | (level == depth - 1)


def refit_kernel(tile, depth, table, half_norms, keep, got, came, passed, *refs):
    over_came, over_passed, refined, rows, scores, sums = refs
    feature_dim = table.shape[1]
    mine = chip_place()[2]
    end, here = end_chip(depth), came_to(1, depth)
    sums[...] = keep[...] + got[...]

    def add(*parts):
        add_rows(table, half_norms, parts, rows, scores, ((mine, sums),), tile)

    @pl.when(end & here)
    def _():
        gather_rows((came, over_came), rows)

    @pl.when(end & jnp.logical_not(here))
    def _():
        gather_rows((passed, over_passed), rows)

    @pl.when(jnp.logical_not(end))
    def _():
        gather_rows((came, passed), rows)

    add(rows)
    old = table[at_tile(mine, tile), :].astype(jnp.float32)
    scale = 1.0 / (sums[:, feature_dim : feature_dim + 1] + 1.0)
    refined[...] = ((sums[:, :feature_dim] + old) * scale).astype(jnp.bfloat16)


def cost(flops=1 << 20):
    return pl.CostEstimate(flops=flops, bytes_accessed=0, transcendentals=0)


def handoff(points, centroids, dest_group):
    group_count = lax.axis_size("group")
    member_count = lax.axis_size("member")
    depth = member_count // 2
    row_count, feature_dim = points.shape
    fine_count = centroids.shape[0]
    tile = fine_count // member_count

    def swap(x):
        return lax.ppermute(x, "member", [(i, i ^ 1) for i in range(member_count)])

    def along(x, moves):
        up = [(2 * z, 2 * to) for z, to in moves]
        down = [(2 * (depth - 1 - z) + 1, 2 * (depth - 1 - to) + 1) for z, to in moves]
        return lax.ppermute(x, "member", up + down)

    last = depth - 1
    apart = [(0, last - 1), (last - 1, last)]
    over = [(1, last)]
    beside = [(z, z + 1) for z in range(last)]

    sums_shape = jax.ShapeDtypeStruct((tile, feature_dim + lanes), jnp.float32)
    norms_shape = jax.ShapeDtypeStruct((fine_count, 1), jnp.float32)

    def kernel(body, out_shape, *operands, scratch=(), aliases={}, flops=1 << 28, specs=()):
        return pl.pallas_call(
            body,
            out_shape=out_shape,
            in_specs=list(specs) + [vmem()] * (len(operands) - len(specs)),
            out_specs=jax.tree.map(lambda _: vmem(), out_shape),
            scratch_shapes=scratch,
            input_output_aliases=aliases,
            compiler_params=pltpu.CompilerParams(vmem_limit_bytes=vmem_limit),
            cost_estimate=cost(flops),
            name=body.func.__name__,
        )(*operands)

    def scratch(rows):
        return [
            pltpu.VMEM((rows, feature_dim), jnp.bfloat16),
            pltpu.VMEM((fine_count, rows), jnp.float32),
        ]

    packed = pack(dest_group.reshape(1, row_count), points, group_count)
    fetched = [
        lax.ppermute(packed[k], "group", [(i, i ^ k) for i in range(group_count)])
        for k in reversed(range(1, group_count))
    ]
    near = join([packed[0], swap(packed[0])])
    apart_near, over_near = along(near, apart), along(near, over)
    first = join(fetched)
    apart_first = along(first, apart)
    swapped = [swap(rows) for rows in fetched]
    second = join(swapped)
    apart_second = along(second, apart)
    over_first = along(join(fetched + swapped[:1]), over)
    two_sums = [sums_shape, sums_shape]
    table, keep, give, half_norms = kernel(
        functools.partial(first_kernel, tile, depth),
        [like(centroids), *two_sums, norms_shape],
        pltpu.with_memory_space_constraint(centroids, pltpu.HBM),
        packed[0],
        first,
        apart_near,
        over_near,
        scratch=[pltpu.SemaphoreType.DMA((member_count,)), *scratch(row_count + 2 * near.shape[0])],
        flops=own_flops,
        specs=[hbm()],
    )

    def add(body, keep, give, *parts, flops=1 << 28):
        return kernel(
            body,
            two_sums,
            table,
            half_norms,
            keep,
            give,
            *parts,
            scratch=scratch(sum(part.shape[0] for part in parts)),
            aliases={2: 0, 3: 1},
            flops=flops,
        )

    beside_first = along(pick(depth, first, apart_first, keep), beside)
    beside_second = along(pick(depth, second, apart_second, keep), beside)
    beside_near = along(pick(depth, near, apart_near, keep), beside)
    over_second = along(join(swapped[1:]), over)
    own_body = functools.partial(own_kernel, tile, depth)
    keep, give = add(own_body, keep, give, packed[0], first, apart_near, apart_first, apart_second)
    over_body = functools.partial(step_kernel, tile, depth, last)
    keep, give = add(over_body, keep, give, over_first)
    beside_body = functools.partial(step_kernel, tile, depth, 1)
    keep, give = add(beside_body, keep, give, beside_first, flops=beside_flops)
    keep, give = add(beside_body, keep, give, beside_second)
    got = jnp.concatenate([swap(give[: tile // 2]), swap(give[tile // 2 :])], axis=0)
    over_last = join([over_second], keep, flops=over_flops)
    beside_last = join([beside_near], keep, flops=last_flops)
    return kernel(
        functools.partial(refit_kernel, tile, depth),
        jax.ShapeDtypeStruct((tile, feature_dim), jnp.bfloat16),
        table,
        half_norms,
        keep,
        got,
        beside_last,
        swap(beside_last),
        over_last,
        swap(over_last),
        scratch=scratch(2 * near.shape[0]) + [pltpu.VMEM(sums_shape.shape, jnp.float32)],
    )


def solution(mesh):
    def local(points, centroids, dest_group):
        groups, members = mesh.shape["group"], mesh.shape["member"]
        if groups * (points.shape[0] // 4) == points.shape[0] and members // 2 == 4:
            return handoff(points, centroids, dest_group)
        return general(points, centroids, dest_group)

    return jax.shard_map(
        local,
        mesh=mesh,
        in_specs=(P(("group", "member"), None), P("group", None), P(("group", "member"), None)),
        out_specs=P(("group", "member"), None),
        check_vma=False,
    )
```

```python
import functools
import math

import jax
import jax.numpy as jnp
from jax import lax
from jax.experimental import pallas as pl
from jax.experimental.pallas import tpu as pltpu
from jax.sharding import PartitionSpec as P

score_scale = 0.15
lanes = 128
exponent_scale = score_scale * math.log2(math.e)
own_flops = 1 << 31
beside_flops = 1 << 28
over_flops = 1 << 32
last_flops = 1 << 26
vmem_limit = 20 * 1024 * 1024


def general(points, centroids, dest_group):
    group_count = lax.axis_size("group")
    member_count = lax.axis_size("member")
    point_rows = points.shape[0]
    capacity = point_rows // 4
    feature_dim = points.shape[1]
    fine_count = centroids.shape[0]
    destination = dest_group[:, 0]
    in_group = (destination[:, None] == jnp.arange(group_count, dtype=jnp.int32)[None, :]).astype(
        jnp.int32
    )
    earlier = jnp.cumsum(in_group, axis=0) - in_group
    own_rank = jnp.sum(earlier * in_group, axis=1)
    slot_index = destination * capacity + own_rank
    placement = (
        jnp.arange(group_count * capacity, dtype=jnp.int32)[:, None] == slot_index[None, :]
    ).astype(jnp.bfloat16)
    packed = jnp.dot(placement, points, preferred_element_type=jnp.float32).astype(jnp.bfloat16)
    packed = packed.reshape(group_count, capacity, feature_dim)
    slot_flags = jnp.dot(
        placement, jnp.ones((point_rows, 1), jnp.bfloat16), preferred_element_type=jnp.float32
    )
    slot_flags = slot_flags.astype(jnp.bfloat16).reshape(group_count, capacity, 1)
    centroid_f = centroids.astype(jnp.float32)
    centroid_norms = jnp.sum(centroid_f * centroid_f, axis=1)
    arrived, marks = (
        lax.all_to_all(packed, "group", split_axis=0, concat_axis=0, tiled=True),
        lax.all_to_all(slot_flags, "group", split_axis=0, concat_axis=0, tiled=True),
    )
    rows = arrived.reshape(-1, feature_dim)
    scores = score_scale * (
        jnp.dot(rows, centroids.T, preferred_element_type=jnp.float32)
        - 0.5 * centroid_norms[None, :]
    )
    weights = jax.nn.softmax(scores, axis=-1) * marks.reshape(-1, 1).astype(jnp.float32)
    responsibility = weights.astype(jnp.bfloat16).reshape(
        arrived.shape[0], arrived.shape[1], fine_count
    )
    all_rows = arrived.reshape(-1, feature_dim)
    all_weights = responsibility.reshape(-1, fine_count)
    weighted = jnp.dot(all_weights.T, all_rows, preferred_element_type=jnp.float32)
    soft_counts = jnp.dot(
        jnp.ones((1, all_weights.shape[0]), jnp.bfloat16),
        all_weights,
        preferred_element_type=jnp.float32,
    )[0]
    member_index = lax.axis_index("member")
    tile_sums, tile_counts = (
        lax.psum_scatter(weighted, "member", scatter_dimension=0, tiled=True),
        lax.psum_scatter(soft_counts, "member", scatter_dimension=0, tiled=True),
    )
    tile_rows = fine_count // member_count
    old_tile = lax.dynamic_slice_in_dim(centroid_f, member_index * tile_rows, tile_rows, 0)
    refined = ((tile_sums + old_tile) / (tile_counts + 1.0)[:, None]).astype(jnp.bfloat16)
    return refined


def vmem():
    return pl.BlockSpec(memory_space=pltpu.VMEM)


def hbm():
    return pl.BlockSpec(memory_space=pltpu.HBM)


def unread():
    return pl.BlockSpec(memory_space=pl.ANY)


def like(x):
    return jax.ShapeDtypeStruct(x.shape, x.dtype)


def join_kernel(after_n, *refs):
    gather_rows(refs[after_n:-1], refs[-1])


def join(parts, *after, flops=1 << 20):
    rows = sum(part.shape[0] for part in parts)
    return pl.pallas_call(
        functools.partial(join_kernel, len(after)),
        out_shape=jax.ShapeDtypeStruct((rows, parts[0].shape[1]), parts[0].dtype),
        in_specs=[unread()] * len(after) + [vmem()] * len(parts),
        out_specs=vmem(),
        compiler_params=pltpu.CompilerParams(vmem_limit_bytes=vmem_limit),
        cost_estimate=cost(flops),
        name="join",
    )(*after, *parts)


def pick_kernel(depth, own, came, after, out):
    level, core, _, _ = chip_place()
    forwards = ((core == 0) & (level == depth - 2)) | ((core == 1) & (level == 1))

    @pl.when(forwards)
    def _():
        out[...] = came[...]

    @pl.when(jnp.logical_not(forwards))
    def _():
        out[...] = own[...]


def pick(depth, own, came, after):
    return pl.pallas_call(
        functools.partial(pick_kernel, depth),
        out_shape=like(own),
        in_specs=[vmem(), vmem(), unread()],
        out_specs=vmem(),
        compiler_params=pltpu.CompilerParams(vmem_limit_bytes=vmem_limit),
        cost_estimate=cost(),
        name="pick",
    )(own, came, after)


def pack_kernel(dest_from, points, *refs):
    packed, (dest, rows, dest_arrival, arrival) = refs[:-4], refs[-4:]
    dest_copy = pltpu.make_async_copy(dest_from, dest, dest_arrival)
    dest_copy.start()
    copy = pltpu.make_async_copy(points, rows, arrival)
    copy.start()
    count = len(packed)
    row_count = rows.shape[0]
    capacity = row_count // count
    dest_copy.wait()
    apart = jnp.bitwise_xor(dest[...], lax.axis_index("group"))
    named = lax.broadcasted_iota(jnp.int32, (8, row_count), 0) == apart
    row_at = lax.broadcasted_iota(jnp.int32, (row_count, row_count), 0)
    col_at = lax.broadcasted_iota(jnp.int32, (row_count, row_count), 1)
    before = (row_at < col_at).astype(jnp.bfloat16)
    named = named.astype(jnp.float32)
    earlier = jnp.dot(named.astype(jnp.bfloat16), before, preferred_element_type=jnp.float32)
    rank = jnp.sum(earlier * named, axis=0, keepdims=True)
    slot = apart * capacity + rank.astype(jnp.int32)
    placement = (row_at == slot).astype(jnp.bfloat16)
    copy.wait()
    for k in range(count):
        part = placement[k * capacity : (k + 1) * capacity]
        packed[k][...] = jnp.dot(part, rows[...], preferred_element_type=jnp.float32).astype(
            jnp.bfloat16
        )


def pack(dest_row, points, group_count):
    row_count, feature_dim = points.shape
    capacity = row_count // group_count
    return pl.pallas_call(
        pack_kernel,
        out_shape=[jax.ShapeDtypeStruct((capacity, feature_dim), points.dtype)] * group_count,
        in_specs=[hbm(), hbm()],
        out_specs=[vmem()] * group_count,
        scratch_shapes=[
            pltpu.VMEM((1, row_count), jnp.int32),
            pltpu.VMEM((row_count, feature_dim), points.dtype),
            pltpu.SemaphoreType.DMA,
            pltpu.SemaphoreType.DMA,
        ],
        compiler_params=pltpu.CompilerParams(vmem_limit_bytes=vmem_limit),
        cost_estimate=cost(),
        name="pack",
    )(
        pltpu.with_memory_space_constraint(dest_row, pltpu.HBM),
        pltpu.with_memory_space_constraint(points, pltpu.HBM),
    )


def scaled_scores(table, half_norms, rows):
    dims = (((1,), (1,)), ((), ()))
    product = lax.dot_general(table, rows, dims, preferred_element_type=jnp.float32)
    return exponent_scale * (product - half_norms)


def softmax_terms(table, half_norms, rows, scores, tile):
    row_count = rows.shape[0]
    top = jnp.full((1, row_count), -jnp.inf, jnp.float32)
    total = jnp.zeros((1, row_count), jnp.float32)
    for start in range(0, table.shape[0], tile):
        at = slice(start, start + tile)
        block = scaled_scores(table[at, :], half_norms[at, :], rows)
        scores[at, :] = block
        higher = jnp.maximum(top, jnp.max(block, axis=0, keepdims=True))
        here = jnp.sum(jnp.exp2(block - higher), axis=0, keepdims=True)
        total = total * jnp.exp2(top - higher) + here
        top = higher
    return top, 1.0 / total


def gather_rows(parts, rows):
    start = 0
    for part in parts:
        if part is rows:
            return
        rows[start : start + part.shape[0], :] = part[...]
        start += part.shape[0]


def tile_sums(scores, top, inverse, rows):
    weights = (jnp.exp2(scores - top) * inverse).astype(jnp.bfloat16)
    sums = jnp.dot(weights, rows, preferred_element_type=jnp.float32)
    count = jnp.sum(weights.astype(jnp.float32), axis=1, keepdims=True)
    return sums, jnp.broadcast_to(count, (count.shape[0], lanes))


def at_tile(index, tile):
    return pl.ds(pl.multiple_of(index * tile, tile), tile)


def chip_place():
    member = lax.axis_index("member")
    core = member % 2
    return member // 2, core, member, member + 1 - 2 * core


def add_rows(table, half_norms, parts, rows, scores, sums, tile):
    feature_dim = table.shape[1]
    gather_rows(parts, rows)
    count = sum(part.shape[0] for part in parts)
    all_rows = rows[:count, :]
    scores = scores.at[:, :count]
    terms = softmax_terms(table, half_norms, all_rows, scores, tile)
    for index, out in sums:
        more, count = tile_sums(scores[at_tile(index, tile), :], *terms, all_rows)
        out[:, :feature_dim] += more
        out[:, feature_dim:] += count


def came_to(step, depth):
    level, core, _, _ = chip_place()
    return ((core == 0) & (level >= step)) | ((core == 1) & (level < depth - step))


def first_kernel(tile, depth, table_from, near, far, apart, over, *refs):
    table, keep, give, half_norms, arrivals, rows, scores = refs
    copies = []
    for index in range(arrivals.shape[0]):
        at = pl.ds(index * tile, tile)
        copies.append(pltpu.make_async_copy(table_from.at[at], table.at[at], arrivals.at[index]))
    for copy in copies:
        copy.start()
    keep[...] = jnp.zeros_like(keep)
    give[...] = jnp.zeros_like(give)
    for index, copy in enumerate(copies):
        copy.wait()
        at = slice(index * tile, (index + 1) * tile)
        block = table[at, :].astype(jnp.float32)
        half_norms[at, :] = 0.5 * jnp.sum(block * block, axis=1, keepdims=True)

    @pl.when(came_to(depth - 1, depth))
    def _():
        _, _, mine, other = chip_place()
        parts = (near, far, apart, over)
        add_rows(table, half_norms, parts, rows, scores, ((mine, keep), (other, give)), tile)


def own_kernel(tile, depth, table, half_norms, keep_in, give_in, near, far, apart_near, *refs):
    came, (keep, give, rows, scores) = refs[:-4], refs[-4:]
    keep[...] = keep_in[...]
    give[...] = give_in[...]
    _, _, mine, other = chip_place()

    def add(*parts):
        add_rows(table, half_norms, parts, rows, scores, ((mine, keep), (other, give)), tile)

    end, here = came_to(depth - 1, depth), came_to(depth - 2, depth)

    @pl.when(end)
    def _():
        add(*came)

    @pl.when(here & jnp.logical_not(end))
    def _():
        add(near, far, apart_near, *came)

    @pl.when(jnp.logical_not(here))
    def _():
        add(near, far)


def step_kernel(tile, depth, step, table, half_norms, keep_in, give_in, *refs):
    parts, (keep, give, rows, scores) = refs[:-4], refs[-4:]
    keep[...] = keep_in[...]
    give[...] = give_in[...]

    @pl.when(came_to(step, depth))
    def _():
        _, _, mine, other = chip_place()
        add_rows(table, half_norms, parts, rows, scores, ((mine, keep), (other, give)), tile)


def end_chip(depth):
    level = chip_place()[0]
    return (level == 0) | (level == depth - 1)


def base_kernel(tile, table, keep, *refs):
    parts, base = refs[:-1], refs[-1]
    feature_dim = table.shape[1]
    mine = chip_place()[2]
    start = 0
    for got in parts:
        rows = got.shape[0]
        span = slice(start, start + rows)
        old = table[pl.ds(pl.multiple_of(mine * tile + start, rows), rows), :].astype(jnp.float32)
        base[span, :feature_dim] = keep[span, :feature_dim] + got[:, :feature_dim] + old
        base[span, feature_dim:] = keep[span, feature_dim:] + got[:, feature_dim:] + 1.0
        start += rows


def refit_kernel(tile, depth, table, half_norms, base, came, passed, *refs):
    over_came, over_passed, refined, rows, scores, out, sent = refs
    feature_dim = table.shape[1]
    mine = chip_place()[2]
    end, here = end_chip(depth), came_to(1, depth)

    @pl.when(end & here)
    def _():
        gather_rows((came, over_came), rows)

    @pl.when(end & jnp.logical_not(here))
    def _():
        gather_rows((passed, over_passed), rows)

    @pl.when(jnp.logical_not(end))
    def _():
        gather_rows((came, passed), rows)

    all_rows = rows[...]
    terms = softmax_terms(table, half_norms, all_rows, scores, tile)
    half = tile // sent.shape[0]
    copies = []
    for index in range(sent.shape[0]):
        span = slice(index * half, (index + 1) * half)
        at = pl.ds(pl.multiple_of(mine * tile + index * half, half), half)
        sums, count = tile_sums(scores[at, :], *terms, all_rows)
        scale = 1.0 / (base[span, feature_dim : feature_dim + 1] + count[:, :1])
        out[span, :] = ((base[span, :feature_dim] + sums) * scale).astype(jnp.bfloat16)
        copies.append(pltpu.make_async_copy(out.at[span], refined.at[span], sent.at[index]))
        copies[-1].start()
    for copy in copies:
        copy.wait()


def cost(flops=1 << 20):
    return pl.CostEstimate(flops=flops, bytes_accessed=0, transcendentals=0)


def handoff(points, centroids, dest_group):
    group_count = lax.axis_size("group")
    member_count = lax.axis_size("member")
    depth = member_count // 2
    row_count, feature_dim = points.shape
    fine_count = centroids.shape[0]
    tile = fine_count // member_count

    def swap(x):
        return lax.ppermute(x, "member", [(i, i ^ 1) for i in range(member_count)])

    def along(x, moves):
        up = [(2 * z, 2 * to) for z, to in moves]
        down = [(2 * (depth - 1 - z) + 1, 2 * (depth - 1 - to) + 1) for z, to in moves]
        return lax.ppermute(x, "member", up + down)

    last = depth - 1
    apart = [(0, last - 1), (last - 1, last)]
    over = [(1, last)]
    beside = [(z, z + 1) for z in range(last)]

    sums_shape = jax.ShapeDtypeStruct((tile, feature_dim + lanes), jnp.float32)
    norms_shape = jax.ShapeDtypeStruct((fine_count, 1), jnp.float32)

    def kernel(body, out_shape, *operands, scratch=(), aliases={}, flops=1 << 28, specs=(), out_specs=None):
        return pl.pallas_call(
            body,
            out_shape=out_shape,
            in_specs=list(specs) + [vmem()] * (len(operands) - len(specs)),
            out_specs=out_specs or jax.tree.map(lambda _: vmem(), out_shape),
            scratch_shapes=scratch,
            input_output_aliases=aliases,
            compiler_params=pltpu.CompilerParams(vmem_limit_bytes=vmem_limit),
            cost_estimate=cost(flops),
            name=body.func.__name__,
        )(*operands)

    def scratch(rows):
        return [
            pltpu.VMEM((rows, feature_dim), jnp.bfloat16),
            pltpu.VMEM((fine_count, rows), jnp.float32),
        ]

    packed = pack(dest_group.reshape(1, row_count), points, group_count)
    fetched = [
        lax.ppermute(packed[k], "group", [(i, i ^ k) for i in range(group_count)])
        for k in reversed(range(1, group_count))
    ]
    near = join([packed[0], swap(packed[0])])
    apart_near, over_near = along(near, apart), along(near, over)
    first = join(fetched)
    apart_first = along(first, apart)
    swapped = [swap(rows) for rows in fetched]
    second = join(swapped)
    apart_second = along(second, apart)
    over_first = along(join(fetched + swapped[:1]), over)
    two_sums = [sums_shape, sums_shape]
    table, keep, give, half_norms = kernel(
        functools.partial(first_kernel, tile, depth),
        [like(centroids), *two_sums, norms_shape],
        pltpu.with_memory_space_constraint(centroids, pltpu.HBM),
        packed[0],
        first,
        apart_near,
        over_near,
        scratch=[pltpu.SemaphoreType.DMA((member_count,)), *scratch(row_count + 2 * near.shape[0])],
        flops=own_flops,
        specs=[hbm()],
    )

    def add(body, keep, give, *parts, flops=1 << 28):
        return kernel(
            body,
            two_sums,
            table,
            half_norms,
            keep,
            give,
            *parts,
            scratch=scratch(sum(part.shape[0] for part in parts)),
            aliases={2: 0, 3: 1},
            flops=flops,
        )

    beside_first = along(pick(depth, first, apart_first, keep), beside)
    beside_second = along(pick(depth, second, apart_second, keep), beside)
    beside_near = along(pick(depth, near, apart_near, keep), beside)
    over_second = along(join(swapped[1:]), over)
    own_body = functools.partial(own_kernel, tile, depth)
    keep, give = add(own_body, keep, give, packed[0], first, apart_near, apart_first, apart_second)
    over_body = functools.partial(step_kernel, tile, depth, last)
    keep, give = add(over_body, keep, give, over_first)
    beside_body = functools.partial(step_kernel, tile, depth, 1)
    keep, give = add(beside_body, keep, give, beside_first, flops=beside_flops)
    keep, give = add(beside_body, keep, give, beside_second)
    base = kernel(
        functools.partial(base_kernel, tile),
        sums_shape,
        table,
        keep,
        swap(give[: tile // 2]),
        swap(give[tile // 2 :]),
        flops=1 << 20,
    )
    over_last = join([over_second], keep, flops=over_flops)
    beside_last = join([beside_near], keep, flops=last_flops)
    return kernel(
        functools.partial(refit_kernel, tile, depth),
        jax.ShapeDtypeStruct((tile, feature_dim), jnp.bfloat16),
        table,
        half_norms,
        base,
        beside_last,
        swap(beside_last),
        over_last,
        swap(over_last),
        scratch=scratch(2 * near.shape[0])
        + [pltpu.VMEM((tile, feature_dim), jnp.bfloat16), pltpu.SemaphoreType.DMA((2,))],
        out_specs=hbm(),
    )


def solution(mesh):
    def local(points, centroids, dest_group):
        groups, members = mesh.shape["group"], mesh.shape["member"]
        if groups * (points.shape[0] // 4) == points.shape[0] and members // 2 == 4:
            return handoff(points, centroids, dest_group)
        return general(points, centroids, dest_group)

    return jax.shard_map(
        local,
        mesh=mesh,
        in_specs=(P(("group", "member"), None), P("group", None), P(("group", "member"), None)),
        out_specs=P(("group", "member"), None),
        check_vma=False,
    )
```

```python
import functools
import math

import jax
import jax.numpy as jnp
from jax import lax
from jax.experimental import pallas as pl
from jax.experimental.pallas import tpu as pltpu
from jax.sharding import PartitionSpec as P

score_scale = 0.15
lanes = 128
exponent_scale = score_scale * math.log2(math.e)
pick_flops = 1 << 30
own_flops = 1 << 31
beside_flops = 1 << 28
over_flops = 1 << 32
last_flops = 1 << 26
vmem_limit = 20 * 1024 * 1024


def general(points, centroids, dest_group):
    group_count = lax.axis_size("group")
    member_count = lax.axis_size("member")
    point_rows = points.shape[0]
    capacity = point_rows // 4
    feature_dim = points.shape[1]
    fine_count = centroids.shape[0]
    destination = dest_group[:, 0]
    in_group = (destination[:, None] == jnp.arange(group_count, dtype=jnp.int32)[None, :]).astype(
        jnp.int32
    )
    earlier = jnp.cumsum(in_group, axis=0) - in_group
    own_rank = jnp.sum(earlier * in_group, axis=1)
    slot_index = destination * capacity + own_rank
    placement = (
        jnp.arange(group_count * capacity, dtype=jnp.int32)[:, None] == slot_index[None, :]
    ).astype(jnp.bfloat16)
    packed = jnp.dot(placement, points, preferred_element_type=jnp.float32).astype(jnp.bfloat16)
    packed = packed.reshape(group_count, capacity, feature_dim)
    slot_flags = jnp.dot(
        placement, jnp.ones((point_rows, 1), jnp.bfloat16), preferred_element_type=jnp.float32
    )
    slot_flags = slot_flags.astype(jnp.bfloat16).reshape(group_count, capacity, 1)
    centroid_f = centroids.astype(jnp.float32)
    centroid_norms = jnp.sum(centroid_f * centroid_f, axis=1)
    arrived, marks = (
        lax.all_to_all(packed, "group", split_axis=0, concat_axis=0, tiled=True),
        lax.all_to_all(slot_flags, "group", split_axis=0, concat_axis=0, tiled=True),
    )
    rows = arrived.reshape(-1, feature_dim)
    scores = score_scale * (
        jnp.dot(rows, centroids.T, preferred_element_type=jnp.float32)
        - 0.5 * centroid_norms[None, :]
    )
    weights = jax.nn.softmax(scores, axis=-1) * marks.reshape(-1, 1).astype(jnp.float32)
    responsibility = weights.astype(jnp.bfloat16).reshape(
        arrived.shape[0], arrived.shape[1], fine_count
    )
    all_rows = arrived.reshape(-1, feature_dim)
    all_weights = responsibility.reshape(-1, fine_count)
    weighted = jnp.dot(all_weights.T, all_rows, preferred_element_type=jnp.float32)
    soft_counts = jnp.dot(
        jnp.ones((1, all_weights.shape[0]), jnp.bfloat16),
        all_weights,
        preferred_element_type=jnp.float32,
    )[0]
    member_index = lax.axis_index("member")
    tile_sums, tile_counts = (
        lax.psum_scatter(weighted, "member", scatter_dimension=0, tiled=True),
        lax.psum_scatter(soft_counts, "member", scatter_dimension=0, tiled=True),
    )
    tile_rows = fine_count // member_count
    old_tile = lax.dynamic_slice_in_dim(centroid_f, member_index * tile_rows, tile_rows, 0)
    refined = ((tile_sums + old_tile) / (tile_counts + 1.0)[:, None]).astype(jnp.bfloat16)
    return refined


def vmem():
    return pl.BlockSpec(memory_space=pltpu.VMEM)


def hbm():
    return pl.BlockSpec(memory_space=pltpu.HBM)


def unread():
    return pl.BlockSpec(memory_space=pl.ANY)


def like(x):
    return jax.ShapeDtypeStruct(x.shape, x.dtype)


def join_kernel(after_n, spans, *refs):
    out, start = refs[-1], 0
    for (low, high), part in zip(spans, refs[after_n:-1]):
        out[start : start + high - low, :] = part[low:high, :]
        start += high - low


def join(parts, *after, flops=1 << 20, spans=None):
    spans = spans or [(0, part.shape[0]) for part in parts]
    rows = sum(high - low for low, high in spans)
    return pl.pallas_call(
        functools.partial(join_kernel, len(after), spans),
        out_shape=jax.ShapeDtypeStruct((rows, parts[0].shape[1]), parts[0].dtype),
        in_specs=[unread()] * len(after) + [vmem()] * len(parts),
        out_specs=vmem(),
        compiler_params=pltpu.CompilerParams(vmem_limit_bytes=vmem_limit),
        cost_estimate=cost(flops),
        name="join",
    )(*after, *parts)


def halve_kernel(whole, upper, lower):
    upper[...] = whole[: upper.shape[0], :]
    lower[...] = whole[upper.shape[0] :, :]


def halve(whole):
    half = jax.ShapeDtypeStruct((whole.shape[0] // 2, whole.shape[1]), whole.dtype)
    return pl.pallas_call(
        halve_kernel,
        out_shape=[half, half],
        in_specs=[vmem()],
        out_specs=[vmem(), vmem()],
        compiler_params=pltpu.CompilerParams(vmem_limit_bytes=vmem_limit),
        cost_estimate=cost(),
        name="halve",
    )(whole)


def pick_kernel(depth, own, came, after, out):
    level, core, _, _ = chip_place()
    forwards = ((core == 0) & (level == depth - 2)) | ((core == 1) & (level == 1))

    @pl.when(forwards)
    def _():
        out[...] = came[...]

    @pl.when(jnp.logical_not(forwards))
    def _():
        out[...] = own[...]


def pick(depth, own, came, after, flops=1 << 20):
    return pl.pallas_call(
        functools.partial(pick_kernel, depth),
        out_shape=like(own),
        in_specs=[vmem(), vmem(), unread()],
        out_specs=vmem(),
        compiler_params=pltpu.CompilerParams(vmem_limit_bytes=vmem_limit),
        cost_estimate=cost(flops),
        name="pick",
    )(own, came, after)


def pack_kernel(dest_from, points, *refs):
    packed, (dest, rows, dest_arrival, arrival) = refs[:-4], refs[-4:]
    dest_copy = pltpu.make_async_copy(dest_from, dest, dest_arrival)
    dest_copy.start()
    copy = pltpu.make_async_copy(points, rows, arrival)
    copy.start()
    count = len(packed)
    row_count = rows.shape[0]
    capacity = row_count // count
    dest_copy.wait()
    apart = jnp.bitwise_xor(dest[...], lax.axis_index("group"))
    named = lax.broadcasted_iota(jnp.int32, (8, row_count), 0) == apart
    row_at = lax.broadcasted_iota(jnp.int32, (row_count, row_count), 0)
    col_at = lax.broadcasted_iota(jnp.int32, (row_count, row_count), 1)
    before = (row_at < col_at).astype(jnp.bfloat16)
    named = named.astype(jnp.float32)
    earlier = jnp.dot(named.astype(jnp.bfloat16), before, preferred_element_type=jnp.float32)
    rank = jnp.sum(earlier * named, axis=0, keepdims=True)
    slot = apart * capacity + rank.astype(jnp.int32)
    placement = (row_at == slot).astype(jnp.bfloat16)
    copy.wait()
    for k in range(count):
        part = placement[k * capacity : (k + 1) * capacity]
        packed[k][...] = jnp.dot(part, rows[...], preferred_element_type=jnp.float32).astype(
            jnp.bfloat16
        )


def pack(dest_row, points, group_count):
    row_count, feature_dim = points.shape
    capacity = row_count // group_count
    return pl.pallas_call(
        pack_kernel,
        out_shape=[jax.ShapeDtypeStruct((capacity, feature_dim), points.dtype)] * group_count,
        in_specs=[hbm(), hbm()],
        out_specs=[vmem()] * group_count,
        scratch_shapes=[
            pltpu.VMEM((1, row_count), jnp.int32),
            pltpu.VMEM((row_count, feature_dim), points.dtype),
            pltpu.SemaphoreType.DMA,
            pltpu.SemaphoreType.DMA,
        ],
        compiler_params=pltpu.CompilerParams(vmem_limit_bytes=vmem_limit),
        cost_estimate=cost(),
        name="pack",
    )(
        pltpu.with_memory_space_constraint(dest_row, pltpu.HBM),
        pltpu.with_memory_space_constraint(points, pltpu.HBM),
    )


def scaled_scores(table, half_norms, rows):
    dims = (((1,), (1,)), ((), ()))
    product = lax.dot_general(table, rows, dims, preferred_element_type=jnp.float32)
    return exponent_scale * (product - half_norms)


def softmax_terms(table, half_norms, rows, scores, tile):
    row_count = rows.shape[0]
    top = jnp.full((1, row_count), -jnp.inf, jnp.float32)
    total = jnp.zeros((1, row_count), jnp.float32)
    for start in range(0, table.shape[0], tile):
        at = slice(start, start + tile)
        block = scaled_scores(table[at, :], half_norms[at, :], rows)
        scores[at, :] = block
        higher = jnp.maximum(top, jnp.max(block, axis=0, keepdims=True))
        here = jnp.sum(jnp.exp2(block - higher), axis=0, keepdims=True)
        total = total * jnp.exp2(top - higher) + here
        top = higher
    return top, 1.0 / total


def gather_rows(parts, rows):
    start = 0
    for part in parts:
        if part is rows:
            return
        rows[start : start + part.shape[0], :] = part[...]
        start += part.shape[0]


def tile_sums(scores, top, inverse, rows):
    weights = (jnp.exp2(scores - top) * inverse).astype(jnp.bfloat16)
    sums = jnp.dot(weights, rows, preferred_element_type=jnp.float32)
    count = jnp.sum(weights.astype(jnp.float32), axis=1, keepdims=True)
    return sums, jnp.broadcast_to(count, (count.shape[0], lanes))


def at_tile(index, tile):
    return pl.ds(pl.multiple_of(index * tile, tile), tile)


def chip_place():
    member = lax.axis_index("member")
    core = member % 2
    return member // 2, core, member, member + 1 - 2 * core


def add_rows(table, half_norms, parts, rows, scores, sums, tile):
    feature_dim = table.shape[1]
    gather_rows(parts, rows)
    count = sum(part.shape[0] for part in parts)
    all_rows = rows[:count, :]
    scores = scores.at[:, :count]
    terms = softmax_terms(table, half_norms, all_rows, scores, tile)
    for index, out in sums:
        more, count = tile_sums(scores[at_tile(index, tile), :], *terms, all_rows)
        out[:, :feature_dim] += more
        out[:, feature_dim:] += count


def came_to(step, depth):
    level, core, _, _ = chip_place()
    return ((core == 0) & (level >= step)) | ((core == 1) & (level < depth - step))


def first_kernel(tile, depth, table_from, near, far, over, apart, *refs):
    table, keep, give, half_norms, arrivals, rows, scores = refs
    copies = []
    for index in range(arrivals.shape[0]):
        at = pl.ds(index * tile, tile)
        copies.append(pltpu.make_async_copy(table_from.at[at], table.at[at], arrivals.at[index]))
    for copy in copies:
        copy.start()
    keep[...] = jnp.zeros_like(keep)
    give[...] = jnp.zeros_like(give)
    for index, copy in enumerate(copies):
        copy.wait()
        at = slice(index * tile, (index + 1) * tile)
        block = table[at, :].astype(jnp.float32)
        half_norms[at, :] = 0.5 * jnp.sum(block * block, axis=1, keepdims=True)

    @pl.when(came_to(depth - 1, depth))
    def _():
        _, _, mine, other = chip_place()
        parts = (near, far, apart, over)
        add_rows(table, half_norms, parts, rows, scores, ((mine, keep), (other, give)), tile)


def own_kernel(tile, depth, table, half_norms, keep_in, give_in, near, far, apart_near, *refs):
    came, (keep, give, rows, scores) = refs[:-4], refs[-4:]
    keep[...] = keep_in[...]
    give[...] = give_in[...]
    _, _, mine, other = chip_place()

    def add(*parts):
        add_rows(table, half_norms, parts, rows, scores, ((mine, keep), (other, give)), tile)

    end, here = came_to(depth - 1, depth), came_to(depth - 2, depth)

    @pl.when(end)
    def _():
        add(*came)

    @pl.when(here & jnp.logical_not(end))
    def _():
        add(near, far, apart_near, *came)

    @pl.when(jnp.logical_not(here))
    def _():
        add(near, far)


def step_kernel(tile, depth, step, table, half_norms, keep_in, give_in, *refs):
    parts, (keep, give, rows, scores) = refs[:-4], refs[-4:]
    keep[...] = keep_in[...]
    give[...] = give_in[...]

    @pl.when(came_to(step, depth))
    def _():
        _, _, mine, other = chip_place()
        add_rows(table, half_norms, parts, rows, scores, ((mine, keep), (other, give)), tile)


def end_chip(depth):
    level = chip_place()[0]
    return (level == 0) | (level == depth - 1)


def base_kernel(tile, table, keep, *refs):
    parts, base = refs[:-1], refs[-1]
    feature_dim = table.shape[1]
    mine = chip_place()[2]
    start = 0
    for got in parts:
        rows = got.shape[0]
        span = slice(start, start + rows)
        old = table[pl.ds(pl.multiple_of(mine * tile + start, rows), rows), :].astype(jnp.float32)
        base[span, :feature_dim] = keep[span, :feature_dim] + got[:, :feature_dim] + old
        base[span, feature_dim:] = keep[span, feature_dim:] + got[:, feature_dim:] + 1.0
        start += rows


def refit_kernel(tile, depth, table, half_norms, base, came, passed, *refs):
    over_came, over_passed, refined, rows, scores, out, sent = refs
    feature_dim = table.shape[1]
    mine = chip_place()[2]
    end, here = end_chip(depth), came_to(1, depth)

    @pl.when(end & here)
    def _():
        gather_rows((came, over_came), rows)

    @pl.when(end & jnp.logical_not(here))
    def _():
        gather_rows((passed, over_passed), rows)

    @pl.when(jnp.logical_not(end))
    def _():
        gather_rows((came, passed), rows)

    all_rows = rows[...]
    terms = softmax_terms(table, half_norms, all_rows, scores, tile)
    half = tile // sent.shape[0]
    copies = []
    for index in range(sent.shape[0]):
        span = slice(index * half, (index + 1) * half)
        at = pl.ds(pl.multiple_of(mine * tile + index * half, half), half)
        sums, count = tile_sums(scores[at, :], *terms, all_rows)
        scale = 1.0 / (base[span, feature_dim : feature_dim + 1] + count[:, :1])
        out[span, :] = ((base[span, :feature_dim] + sums) * scale).astype(jnp.bfloat16)
        copies.append(pltpu.make_async_copy(out.at[span], refined.at[span], sent.at[index]))
        copies[-1].start()
    for copy in copies:
        copy.wait()


def cost(flops=1 << 20):
    return pl.CostEstimate(flops=flops, bytes_accessed=0, transcendentals=0)


def handoff(points, centroids, dest_group):
    group_count = lax.axis_size("group")
    member_count = lax.axis_size("member")
    depth = member_count // 2
    row_count, feature_dim = points.shape
    fine_count = centroids.shape[0]
    tile = fine_count // member_count

    def swap(x):
        return lax.ppermute(x, "member", [(i, i ^ 1) for i in range(member_count)])

    def along(x, moves):
        up = [(2 * z, 2 * to) for z, to in moves]
        down = [(2 * (depth - 1 - z) + 1, 2 * (depth - 1 - to) + 1) for z, to in moves]
        return lax.ppermute(x, "member", up + down)

    last = depth - 1
    apart = [(0, last - 1), (last - 1, last)]
    over = [(1, last)]
    beside = [(z, z + 1) for z in range(last)]

    sums_shape = jax.ShapeDtypeStruct((tile, feature_dim + lanes), jnp.float32)
    norms_shape = jax.ShapeDtypeStruct((fine_count, 1), jnp.float32)

    def kernel(body, out_shape, *operands, scratch=(), aliases={}, flops=1 << 28, specs=(), out_specs=None):
        return pl.pallas_call(
            body,
            out_shape=out_shape,
            in_specs=list(specs) + [vmem()] * (len(operands) - len(specs)),
            out_specs=out_specs or jax.tree.map(lambda _: vmem(), out_shape),
            scratch_shapes=scratch,
            input_output_aliases=aliases,
            compiler_params=pltpu.CompilerParams(vmem_limit_bytes=vmem_limit),
            cost_estimate=cost(flops),
            name=body.func.__name__,
        )(*operands)

    def scratch(rows):
        return [
            pltpu.VMEM((rows, feature_dim), jnp.bfloat16),
            pltpu.VMEM((fine_count, rows), jnp.float32),
        ]

    packed = pack(dest_group.reshape(1, row_count), points, group_count)
    fetched = [
        lax.ppermute(packed[k], "group", [(i, i ^ k) for i in range(group_count)])
        for k in reversed(range(1, group_count))
    ]
    near = join([packed[0], swap(packed[0])])
    apart_near, over_near = along(near, apart), along(near, over)
    first = join(fetched)
    slot_rows, far_rows = packed[0].shape[0], first.shape[0]
    apart_first = along(first, apart)
    halves = halve(first)
    swapped = [swap(half) for half in halves]
    second = join(swapped)
    apart_second = along(second, apart)
    over_first = along(join([first, second], spans=[(0, far_rows), (0, slot_rows)]), over)
    two_sums = [sums_shape, sums_shape]
    table, keep, give, half_norms = kernel(
        functools.partial(first_kernel, tile, depth),
        [like(centroids), *two_sums, norms_shape],
        pltpu.with_memory_space_constraint(centroids, pltpu.HBM),
        packed[0],
        first,
        over_near,
        apart_near,
        scratch=[pltpu.SemaphoreType.DMA((member_count,)), *scratch(row_count + 2 * near.shape[0])],
        flops=own_flops,
        specs=[hbm()],
    )

    def add(body, keep, give, *parts, flops=1 << 28):
        return kernel(
            body,
            two_sums,
            table,
            half_norms,
            keep,
            give,
            *parts,
            scratch=scratch(sum(part.shape[0] for part in parts)),
            aliases={2: 0, 3: 1},
            flops=flops,
        )

    beside_first = along(pick(depth, first, apart_first, keep, pick_flops), beside)
    beside_second = along(pick(depth, second, apart_second, keep), beside)
    beside_near = along(pick(depth, near, apart_near, keep), beside)
    over_second = along(join([second], spans=[(slot_rows, far_rows)]), over)
    own_body = functools.partial(own_kernel, tile, depth)
    keep, give = add(own_body, keep, give, packed[0], first, apart_near, apart_first, apart_second)
    over_body = functools.partial(step_kernel, tile, depth, last)
    keep, give = add(over_body, keep, give, over_first)
    beside_body = functools.partial(step_kernel, tile, depth, 1)
    keep, give = add(beside_body, keep, give, beside_first, flops=beside_flops)
    keep, give = add(beside_body, keep, give, beside_second)
    base = kernel(
        functools.partial(base_kernel, tile),
        sums_shape,
        table,
        keep,
        swap(give[: tile // 2]),
        swap(give[tile // 2 :]),
        flops=1 << 20,
    )
    over_last = join([over_second], keep, flops=over_flops)
    beside_last = join([beside_near], keep, flops=last_flops)
    return kernel(
        functools.partial(refit_kernel, tile, depth),
        jax.ShapeDtypeStruct((tile, feature_dim), jnp.bfloat16),
        table,
        half_norms,
        base,
        beside_last,
        swap(beside_last),
        over_last,
        swap(over_last),
        scratch=scratch(2 * near.shape[0])
        + [pltpu.VMEM((tile, feature_dim), jnp.bfloat16), pltpu.SemaphoreType.DMA((2,))],
        out_specs=hbm(),
    )


def solution(mesh):
    def local(points, centroids, dest_group):
        groups, members = mesh.shape["group"], mesh.shape["member"]
        if groups * (points.shape[0] // 4) == points.shape[0] and members // 2 == 4:
            return handoff(points, centroids, dest_group)
        return general(points, centroids, dest_group)

    return jax.shard_map(
        local,
        mesh=mesh,
        in_specs=(P(("group", "member"), None), P("group", None), P(("group", "member"), None)),
        out_specs=P(("group", "member"), None),
        check_vma=False,
    )
```

```python
import functools
import math

import jax
import jax.numpy as jnp
from jax import lax
from jax.experimental import pallas as pl
from jax.experimental.pallas import tpu as pltpu
from jax.sharding import PartitionSpec as P

score_scale = 0.15
lanes = 128
exponent_scale = score_scale * math.log2(math.e)
pick_flops = 1 << 30
own_flops = 1 << 31
beside_flops = 1 << 28
over_flops = 1 << 32
last_flops = 1 << 26
vmem_limit = 20 * 1024 * 1024


def general(points, centroids, dest_group):
    group_count = lax.axis_size("group")
    member_count = lax.axis_size("member")
    point_rows = points.shape[0]
    capacity = point_rows // 4
    feature_dim = points.shape[1]
    fine_count = centroids.shape[0]
    destination = dest_group[:, 0]
    in_group = (destination[:, None] == jnp.arange(group_count, dtype=jnp.int32)[None, :]).astype(
        jnp.int32
    )
    earlier = jnp.cumsum(in_group, axis=0) - in_group
    own_rank = jnp.sum(earlier * in_group, axis=1)
    slot_index = destination * capacity + own_rank
    placement = (
        jnp.arange(group_count * capacity, dtype=jnp.int32)[:, None] == slot_index[None, :]
    ).astype(jnp.bfloat16)
    packed = jnp.dot(placement, points, preferred_element_type=jnp.float32).astype(jnp.bfloat16)
    packed = packed.reshape(group_count, capacity, feature_dim)
    slot_flags = jnp.dot(
        placement, jnp.ones((point_rows, 1), jnp.bfloat16), preferred_element_type=jnp.float32
    )
    slot_flags = slot_flags.astype(jnp.bfloat16).reshape(group_count, capacity, 1)
    centroid_f = centroids.astype(jnp.float32)
    centroid_norms = jnp.sum(centroid_f * centroid_f, axis=1)
    arrived, marks = (
        lax.all_to_all(packed, "group", split_axis=0, concat_axis=0, tiled=True),
        lax.all_to_all(slot_flags, "group", split_axis=0, concat_axis=0, tiled=True),
    )
    rows = arrived.reshape(-1, feature_dim)
    scores = score_scale * (
        jnp.dot(rows, centroids.T, preferred_element_type=jnp.float32)
        - 0.5 * centroid_norms[None, :]
    )
    weights = jax.nn.softmax(scores, axis=-1) * marks.reshape(-1, 1).astype(jnp.float32)
    responsibility = weights.astype(jnp.bfloat16).reshape(
        arrived.shape[0], arrived.shape[1], fine_count
    )
    all_rows = arrived.reshape(-1, feature_dim)
    all_weights = responsibility.reshape(-1, fine_count)
    weighted = jnp.dot(all_weights.T, all_rows, preferred_element_type=jnp.float32)
    soft_counts = jnp.dot(
        jnp.ones((1, all_weights.shape[0]), jnp.bfloat16),
        all_weights,
        preferred_element_type=jnp.float32,
    )[0]
    member_index = lax.axis_index("member")
    tile_sums, tile_counts = (
        lax.psum_scatter(weighted, "member", scatter_dimension=0, tiled=True),
        lax.psum_scatter(soft_counts, "member", scatter_dimension=0, tiled=True),
    )
    tile_rows = fine_count // member_count
    old_tile = lax.dynamic_slice_in_dim(centroid_f, member_index * tile_rows, tile_rows, 0)
    refined = ((tile_sums + old_tile) / (tile_counts + 1.0)[:, None]).astype(jnp.bfloat16)
    return refined


def vmem():
    return pl.BlockSpec(memory_space=pltpu.VMEM)


def hbm():
    return pl.BlockSpec(memory_space=pltpu.HBM)


def unread():
    return pl.BlockSpec(memory_space=pl.ANY)


def like(x):
    return jax.ShapeDtypeStruct(x.shape, x.dtype)


def join_kernel(after_n, spans, *refs):
    out, start = refs[-1], 0
    for (low, high), part in zip(spans, refs[after_n:-1]):
        out[start : start + high - low, :] = part[low:high, :]
        start += high - low


def join(parts, *after, flops=1 << 20, spans=None):
    spans = spans or [(0, part.shape[0]) for part in parts]
    rows = sum(high - low for low, high in spans)
    return pl.pallas_call(
        functools.partial(join_kernel, len(after), spans),
        out_shape=jax.ShapeDtypeStruct((rows, parts[0].shape[1]), parts[0].dtype),
        in_specs=[unread()] * len(after) + [vmem()] * len(parts),
        out_specs=vmem(),
        compiler_params=pltpu.CompilerParams(vmem_limit_bytes=vmem_limit),
        cost_estimate=cost(flops),
        name="join",
    )(*after, *parts)


def halve_kernel(whole, upper, lower):
    upper[...] = whole[: upper.shape[0], :]
    lower[...] = whole[upper.shape[0] :, :]


def halve(whole):
    half = jax.ShapeDtypeStruct((whole.shape[0] // 2, whole.shape[1]), whole.dtype)
    return pl.pallas_call(
        halve_kernel,
        out_shape=[half, half],
        in_specs=[vmem()],
        out_specs=[vmem(), vmem()],
        compiler_params=pltpu.CompilerParams(vmem_limit_bytes=vmem_limit),
        cost_estimate=cost(),
        name="halve",
    )(whole)


def pick_kernel(depth, own, came, after, out):
    level, core, _, _ = chip_place()
    forwards = ((core == 0) & (level == depth - 2)) | ((core == 1) & (level == 1))

    @pl.when(forwards)
    def _():
        out[...] = came[...]

    @pl.when(jnp.logical_not(forwards))
    def _():
        out[...] = own[...]


def pick(depth, own, came, after, flops=1 << 20):
    return pl.pallas_call(
        functools.partial(pick_kernel, depth),
        out_shape=like(own),
        in_specs=[vmem(), vmem(), unread()],
        out_specs=vmem(),
        compiler_params=pltpu.CompilerParams(vmem_limit_bytes=vmem_limit),
        cost_estimate=cost(flops),
        name="pick",
    )(own, came, after)


def pack_kernel(dest_from, points, *refs):
    packed, (dest, rows, dest_arrival, arrival) = refs[:-4], refs[-4:]
    dest_copy = pltpu.make_async_copy(dest_from, dest, dest_arrival)
    dest_copy.start()
    copy = pltpu.make_async_copy(points, rows, arrival)
    copy.start()
    count = len(packed)
    row_count = rows.shape[0]
    capacity = row_count // count
    dest_copy.wait()
    apart = jnp.bitwise_xor(dest[...], lax.axis_index("group"))
    named = lax.broadcasted_iota(jnp.int32, (8, row_count), 0) == apart
    row_at = lax.broadcasted_iota(jnp.int32, (row_count, row_count), 0)
    col_at = lax.broadcasted_iota(jnp.int32, (row_count, row_count), 1)
    before = (row_at < col_at).astype(jnp.bfloat16)
    named = named.astype(jnp.float32)
    earlier = jnp.dot(named.astype(jnp.bfloat16), before, preferred_element_type=jnp.float32)
    rank = jnp.sum(earlier * named, axis=0, keepdims=True)
    slot = apart * capacity + rank.astype(jnp.int32)
    placement = (row_at == slot).astype(jnp.bfloat16)
    copy.wait()
    for k in range(count):
        part = placement[k * capacity : (k + 1) * capacity]
        packed[k][...] = jnp.dot(part, rows[...], preferred_element_type=jnp.float32).astype(
            jnp.bfloat16
        )


def pack(dest_row, points, group_count):
    row_count, feature_dim = points.shape
    capacity = row_count // group_count
    return pl.pallas_call(
        pack_kernel,
        out_shape=[jax.ShapeDtypeStruct((capacity, feature_dim), points.dtype)] * group_count,
        in_specs=[hbm(), hbm()],
        out_specs=[vmem()] * group_count,
        scratch_shapes=[
            pltpu.VMEM((1, row_count), jnp.int32),
            pltpu.VMEM((row_count, feature_dim), points.dtype),
            pltpu.SemaphoreType.DMA,
            pltpu.SemaphoreType.DMA,
        ],
        compiler_params=pltpu.CompilerParams(vmem_limit_bytes=vmem_limit),
        cost_estimate=cost(),
        name="pack",
    )(
        pltpu.with_memory_space_constraint(dest_row, pltpu.HBM),
        pltpu.with_memory_space_constraint(points, pltpu.HBM),
    )


def scaled_scores(table, half_norms, rows):
    dims = (((1,), (1,)), ((), ()))
    product = lax.dot_general(table, rows, dims, preferred_element_type=jnp.float32)
    return exponent_scale * (product - half_norms)


def softmax_terms(table, half_norms, rows, scores, tile):
    row_count = rows.shape[0]
    top = jnp.full((1, row_count), -jnp.inf, jnp.float32)
    total = jnp.zeros((1, row_count), jnp.float32)
    for start in range(0, table.shape[0], tile):
        at = slice(start, start + tile)
        block = scaled_scores(table[at, :], half_norms[at, :], rows)
        scores[at, :] = block
        higher = jnp.maximum(top, jnp.max(block, axis=0, keepdims=True))
        here = jnp.sum(jnp.exp2(block - higher), axis=0, keepdims=True)
        total = total * jnp.exp2(top - higher) + here
        top = higher
    return top, 1.0 / total


def gather_rows(parts, rows):
    start = 0
    for part in parts:
        if part is rows:
            return
        rows[start : start + part.shape[0], :] = part[...]
        start += part.shape[0]


def tile_sums(scores, top, inverse, rows):
    weights = (jnp.exp2(scores - top) * inverse).astype(jnp.bfloat16)
    sums = jnp.dot(weights, rows, preferred_element_type=jnp.float32)
    count = jnp.sum(weights.astype(jnp.float32), axis=1, keepdims=True)
    return sums, jnp.broadcast_to(count, (count.shape[0], lanes))


def at_tile(index, tile):
    return pl.ds(pl.multiple_of(index * tile, tile), tile)


def chip_place():
    member = lax.axis_index("member")
    core = member % 2
    return member // 2, core, member, member + 1 - 2 * core


def add_rows(table, half_norms, parts, rows, scores, sums, tile):
    feature_dim = table.shape[1]
    gather_rows(parts, rows)
    count = sum(part.shape[0] for part in parts)
    all_rows = rows[:count, :]
    scores = scores.at[:, :count]
    terms = softmax_terms(table, half_norms, all_rows, scores, tile)
    for index, out in sums:
        more, count = tile_sums(scores[at_tile(index, tile), :], *terms, all_rows)
        out[:, :feature_dim] += more
        out[:, feature_dim:] += count


def came_to(step, depth):
    level, core, _, _ = chip_place()
    return ((core == 0) & (level >= step)) | ((core == 1) & (level < depth - step))


def first_kernel(tile, depth, table_from, near, far, over, apart, *refs):
    table, keep, give, half_norms, arrivals, rows, scores = refs
    copies = []
    for index in range(arrivals.shape[0]):
        at = pl.ds(index * tile, tile)
        copies.append(pltpu.make_async_copy(table_from.at[at], table.at[at], arrivals.at[index]))
    for copy in copies:
        copy.start()
    keep[...] = jnp.zeros_like(keep)
    give[...] = jnp.zeros_like(give)
    for index, copy in enumerate(copies):
        copy.wait()
        at = slice(index * tile, (index + 1) * tile)
        block = table[at, :].astype(jnp.float32)
        half_norms[at, :] = 0.5 * jnp.sum(block * block, axis=1, keepdims=True)

    @pl.when(came_to(depth - 1, depth))
    def _():
        _, _, mine, other = chip_place()
        parts = (near, far, apart, over)
        add_rows(table, half_norms, parts, rows, scores, ((mine, keep), (other, give)), tile)


def own_kernel(tile, depth, table, half_norms, keep_in, give_in, near, far, over_near, *refs):
    came, (keep, give, rows, scores) = refs[:-4], refs[-4:]
    keep[...] = keep_in[...]
    give[...] = give_in[...]
    _, _, mine, other = chip_place()

    def add(*parts):
        add_rows(table, half_norms, parts, rows, scores, ((mine, keep), (other, give)), tile)

    end, here = came_to(depth - 1, depth), came_to(depth - 2, depth)

    @pl.when(end)
    def _():
        add(*came)

    @pl.when(here & jnp.logical_not(end))
    def _():
        add(near, far, over_near, *came)

    @pl.when(jnp.logical_not(here))
    def _():
        add(near, far)


def step_kernel(tile, depth, step, table, half_norms, keep_in, give_in, *refs):
    parts, (keep, give, rows, scores) = refs[:-4], refs[-4:]
    keep[...] = keep_in[...]
    give[...] = give_in[...]

    @pl.when(came_to(step, depth))
    def _():
        _, _, mine, other = chip_place()
        add_rows(table, half_norms, parts, rows, scores, ((mine, keep), (other, give)), tile)


def end_chip(depth):
    level = chip_place()[0]
    return (level == 0) | (level == depth - 1)


def base_kernel(tile, table, keep, *refs):
    parts, base = refs[:-1], refs[-1]
    feature_dim = table.shape[1]
    mine = chip_place()[2]
    start = 0
    for got in parts:
        rows = got.shape[0]
        span = slice(start, start + rows)
        old = table[pl.ds(pl.multiple_of(mine * tile + start, rows), rows), :].astype(jnp.float32)
        base[span, :feature_dim] = keep[span, :feature_dim] + got[:, :feature_dim] + old
        base[span, feature_dim:] = keep[span, feature_dim:] + got[:, feature_dim:] + 1.0
        start += rows


def refit_kernel(tile, depth, table, half_norms, base, came, passed, *refs):
    over_came, over_passed, refined, rows, scores, out, sent = refs
    feature_dim = table.shape[1]
    mine = chip_place()[2]
    end, here = end_chip(depth), came_to(1, depth)

    @pl.when(end & here)
    def _():
        gather_rows((came, over_came), rows)

    @pl.when(end & jnp.logical_not(here))
    def _():
        gather_rows((passed, over_passed), rows)

    @pl.when(jnp.logical_not(end))
    def _():
        gather_rows((came, passed), rows)

    all_rows = rows[...]
    terms = softmax_terms(table, half_norms, all_rows, scores, tile)
    half = tile // sent.shape[0]
    copies = []
    for index in range(sent.shape[0]):
        span = slice(index * half, (index + 1) * half)
        at = pl.ds(pl.multiple_of(mine * tile + index * half, half), half)
        sums, count = tile_sums(scores[at, :], *terms, all_rows)
        scale = 1.0 / (base[span, feature_dim : feature_dim + 1] + count[:, :1])
        out[span, :] = ((base[span, :feature_dim] + sums) * scale).astype(jnp.bfloat16)
        copies.append(pltpu.make_async_copy(out.at[span], refined.at[span], sent.at[index]))
        copies[-1].start()
    for copy in copies:
        copy.wait()


def cost(flops=1 << 20):
    return pl.CostEstimate(flops=flops, bytes_accessed=0, transcendentals=0)


def handoff(points, centroids, dest_group):
    group_count = lax.axis_size("group")
    member_count = lax.axis_size("member")
    depth = member_count // 2
    row_count, feature_dim = points.shape
    fine_count = centroids.shape[0]
    tile = fine_count // member_count

    def swap(x):
        return lax.ppermute(x, "member", [(i, i ^ 1) for i in range(member_count)])

    def along(x, moves):
        up = [(2 * z, 2 * to) for z, to in moves]
        down = [(2 * (depth - 1 - z) + 1, 2 * (depth - 1 - to) + 1) for z, to in moves]
        return lax.ppermute(x, "member", up + down)

    last = depth - 1
    apart = [(0, last - 1), (last - 1, last)]
    over = [(1, last)]
    beside = [(z, z + 1) for z in range(last)]

    sums_shape = jax.ShapeDtypeStruct((tile, feature_dim + lanes), jnp.float32)
    norms_shape = jax.ShapeDtypeStruct((fine_count, 1), jnp.float32)

    def kernel(body, out_shape, *operands, scratch=(), aliases={}, flops=1 << 28, specs=(), out_specs=None):
        return pl.pallas_call(
            body,
            out_shape=out_shape,
            in_specs=list(specs) + [vmem()] * (len(operands) - len(specs)),
            out_specs=out_specs or jax.tree.map(lambda _: vmem(), out_shape),
            scratch_shapes=scratch,
            input_output_aliases=aliases,
            compiler_params=pltpu.CompilerParams(vmem_limit_bytes=vmem_limit),
            cost_estimate=cost(flops),
            name=body.func.__name__,
        )(*operands)

    def scratch(rows):
        return [
            pltpu.VMEM((rows, feature_dim), jnp.bfloat16),
            pltpu.VMEM((fine_count, rows), jnp.float32),
        ]

    packed = pack(dest_group.reshape(1, row_count), points, group_count)
    fetched = [
        lax.ppermute(packed[k], "group", [(i, i ^ k) for i in range(group_count)])
        for k in reversed(range(1, group_count))
    ]
    near = join([packed[0], swap(packed[0])])
    apart_near, over_near = along(near, apart[1:]), along(near, over + apart[:1])
    first = join(fetched)
    slot_rows, far_rows = packed[0].shape[0], first.shape[0]
    apart_first = along(first, apart)
    halves = halve(first)
    swapped = [swap(half) for half in halves]
    second = join(swapped)
    apart_second = along(second, apart)
    over_first = along(join([first, second], spans=[(0, far_rows), (0, slot_rows)]), over)
    two_sums = [sums_shape, sums_shape]
    table, keep, give, half_norms = kernel(
        functools.partial(first_kernel, tile, depth),
        [like(centroids), *two_sums, norms_shape],
        pltpu.with_memory_space_constraint(centroids, pltpu.HBM),
        packed[0],
        first,
        over_near,
        apart_near,
        scratch=[pltpu.SemaphoreType.DMA((member_count,)), *scratch(row_count + 2 * near.shape[0])],
        flops=own_flops,
        specs=[hbm()],
    )

    def add(body, keep, give, *parts, flops=1 << 28):
        return kernel(
            body,
            two_sums,
            table,
            half_norms,
            keep,
            give,
            *parts,
            scratch=scratch(sum(part.shape[0] for part in parts)),
            aliases={2: 0, 3: 1},
            flops=flops,
        )

    beside_first = along(pick(depth, first, apart_first, keep, pick_flops), beside)
    beside_second = along(pick(depth, second, apart_second, keep), beside)
    beside_near = along(pick(depth, near, over_near, keep), beside)
    over_second = along(join([second], spans=[(slot_rows, far_rows)]), over)
    own_body = functools.partial(own_kernel, tile, depth)
    keep, give = add(own_body, keep, give, packed[0], first, over_near, apart_first, apart_second)
    over_body = functools.partial(step_kernel, tile, depth, last)
    keep, give = add(over_body, keep, give, over_first)
    beside_body = functools.partial(step_kernel, tile, depth, 1)
    keep, give = add(beside_body, keep, give, beside_first, flops=beside_flops)
    keep, give = add(beside_body, keep, give, beside_second)
    base = kernel(
        functools.partial(base_kernel, tile),
        sums_shape,
        table,
        keep,
        swap(give[: tile // 2]),
        swap(give[tile // 2 :]),
        flops=1 << 20,
    )
    over_last = join([over_second], keep, flops=over_flops)
    beside_last = join([beside_near], keep, flops=last_flops)
    return kernel(
        functools.partial(refit_kernel, tile, depth),
        jax.ShapeDtypeStruct((tile, feature_dim), jnp.bfloat16),
        table,
        half_norms,
        base,
        beside_last,
        swap(beside_last),
        over_last,
        swap(over_last),
        scratch=scratch(2 * near.shape[0])
        + [pltpu.VMEM((tile, feature_dim), jnp.bfloat16), pltpu.SemaphoreType.DMA((2,))],
        out_specs=hbm(),
    )


def solution(mesh):
    def local(points, centroids, dest_group):
        groups, members = mesh.shape["group"], mesh.shape["member"]
        if groups * (points.shape[0] // 4) == points.shape[0] and members // 2 == 4:
            return handoff(points, centroids, dest_group)
        return general(points, centroids, dest_group)

    return jax.shard_map(
        local,
        mesh=mesh,
        in_specs=(P(("group", "member"), None), P("group", None), P(("group", "member"), None)),
        out_specs=P(("group", "member"), None),
        check_vma=False,
    )
```

```python
import functools
import math

import jax
import jax.numpy as jnp
from jax import lax
from jax.experimental import pallas as pl
from jax.experimental.pallas import tpu as pltpu
from jax.sharding import PartitionSpec as P

score_scale = 0.15
lanes = 128
exponent_scale = score_scale * math.log2(math.e)
pick_flops = 1 << 30
own_flops = 1 << 31
beside_flops = 1 << 28
over_flops = 1 << 32
last_flops = 1 << 26
vmem_limit = 20 * 1024 * 1024


def general(points, centroids, dest_group):
    group_count = lax.axis_size("group")
    member_count = lax.axis_size("member")
    point_rows = points.shape[0]
    capacity = point_rows // 4
    feature_dim = points.shape[1]
    fine_count = centroids.shape[0]
    destination = dest_group[:, 0]
    in_group = (destination[:, None] == jnp.arange(group_count, dtype=jnp.int32)[None, :]).astype(
        jnp.int32
    )
    earlier = jnp.cumsum(in_group, axis=0) - in_group
    own_rank = jnp.sum(earlier * in_group, axis=1)
    slot_index = destination * capacity + own_rank
    placement = (
        jnp.arange(group_count * capacity, dtype=jnp.int32)[:, None] == slot_index[None, :]
    ).astype(jnp.bfloat16)
    packed = jnp.dot(placement, points, preferred_element_type=jnp.float32).astype(jnp.bfloat16)
    packed = packed.reshape(group_count, capacity, feature_dim)
    slot_flags = jnp.dot(
        placement, jnp.ones((point_rows, 1), jnp.bfloat16), preferred_element_type=jnp.float32
    )
    slot_flags = slot_flags.astype(jnp.bfloat16).reshape(group_count, capacity, 1)
    centroid_f = centroids.astype(jnp.float32)
    centroid_norms = jnp.sum(centroid_f * centroid_f, axis=1)
    arrived, marks = (
        lax.all_to_all(packed, "group", split_axis=0, concat_axis=0, tiled=True),
        lax.all_to_all(slot_flags, "group", split_axis=0, concat_axis=0, tiled=True),
    )
    rows = arrived.reshape(-1, feature_dim)
    scores = score_scale * (
        jnp.dot(rows, centroids.T, preferred_element_type=jnp.float32)
        - 0.5 * centroid_norms[None, :]
    )
    weights = jax.nn.softmax(scores, axis=-1) * marks.reshape(-1, 1).astype(jnp.float32)
    responsibility = weights.astype(jnp.bfloat16).reshape(
        arrived.shape[0], arrived.shape[1], fine_count
    )
    all_rows = arrived.reshape(-1, feature_dim)
    all_weights = responsibility.reshape(-1, fine_count)
    weighted = jnp.dot(all_weights.T, all_rows, preferred_element_type=jnp.float32)
    soft_counts = jnp.dot(
        jnp.ones((1, all_weights.shape[0]), jnp.bfloat16),
        all_weights,
        preferred_element_type=jnp.float32,
    )[0]
    member_index = lax.axis_index("member")
    tile_sums, tile_counts = (
        lax.psum_scatter(weighted, "member", scatter_dimension=0, tiled=True),
        lax.psum_scatter(soft_counts, "member", scatter_dimension=0, tiled=True),
    )
    tile_rows = fine_count // member_count
    old_tile = lax.dynamic_slice_in_dim(centroid_f, member_index * tile_rows, tile_rows, 0)
    refined = ((tile_sums + old_tile) / (tile_counts + 1.0)[:, None]).astype(jnp.bfloat16)
    return refined


def vmem():
    return pl.BlockSpec(memory_space=pltpu.VMEM)


def hbm():
    return pl.BlockSpec(memory_space=pltpu.HBM)


def unread():
    return pl.BlockSpec(memory_space=pl.ANY)


def like(x):
    return jax.ShapeDtypeStruct(x.shape, x.dtype)


def join_kernel(after_n, spans, *refs):
    out, start = refs[-1], 0
    for (low, high), part in zip(spans, refs[after_n:-1]):
        out[start : start + high - low, :] = part[low:high, :]
        start += high - low


def join(parts, *after, flops=1 << 20, spans=None):
    spans = spans or [(0, part.shape[0]) for part in parts]
    rows = sum(high - low for low, high in spans)
    return pl.pallas_call(
        functools.partial(join_kernel, len(after), spans),
        out_shape=jax.ShapeDtypeStruct((rows, parts[0].shape[1]), parts[0].dtype),
        in_specs=[unread()] * len(after) + [vmem()] * len(parts),
        out_specs=vmem(),
        compiler_params=pltpu.CompilerParams(vmem_limit_bytes=vmem_limit),
        cost_estimate=cost(flops),
        name="join",
    )(*after, *parts)


def halve_kernel(whole, upper, lower):
    upper[...] = whole[: upper.shape[0], :]
    lower[...] = whole[upper.shape[0] :, :]


def halve(whole):
    half = jax.ShapeDtypeStruct((whole.shape[0] // 2, whole.shape[1]), whole.dtype)
    return pl.pallas_call(
        halve_kernel,
        out_shape=[half, half],
        in_specs=[vmem()],
        out_specs=[vmem(), vmem()],
        compiler_params=pltpu.CompilerParams(vmem_limit_bytes=vmem_limit),
        cost_estimate=cost(),
        name="halve",
    )(whole)


def pick_kernel(depth, own, came, after, out):
    level, core, _, _ = chip_place()
    forwards = ((core == 0) & (level == depth - 2)) | ((core == 1) & (level == 1))

    @pl.when(forwards)
    def _():
        out[...] = came[...]

    @pl.when(jnp.logical_not(forwards))
    def _():
        out[...] = own[...]


def pick(depth, own, came, after, flops=1 << 20):
    return pl.pallas_call(
        functools.partial(pick_kernel, depth),
        out_shape=like(own),
        in_specs=[vmem(), vmem(), unread()],
        out_specs=vmem(),
        compiler_params=pltpu.CompilerParams(vmem_limit_bytes=vmem_limit),
        cost_estimate=cost(flops),
        name="pick",
    )(own, came, after)


def pack_kernel(dest_from, points, *refs):
    packed, (dest, rows, dest_arrival, arrival) = refs[:-4], refs[-4:]
    dest_copy = pltpu.make_async_copy(dest_from, dest, dest_arrival)
    dest_copy.start()
    copy = pltpu.make_async_copy(points, rows, arrival)
    copy.start()
    count = len(packed)
    row_count = rows.shape[0]
    capacity = row_count // count
    dest_copy.wait()
    apart = jnp.bitwise_xor(dest[...], lax.axis_index("group"))
    named = lax.broadcasted_iota(jnp.int32, (8, row_count), 0) == apart
    row_at = lax.broadcasted_iota(jnp.int32, (row_count, row_count), 0)
    col_at = lax.broadcasted_iota(jnp.int32, (row_count, row_count), 1)
    before = (row_at < col_at).astype(jnp.bfloat16)
    named = named.astype(jnp.float32)
    earlier = jnp.dot(named.astype(jnp.bfloat16), before, preferred_element_type=jnp.float32)
    rank = jnp.sum(earlier * named, axis=0, keepdims=True)
    slot = apart * capacity + rank.astype(jnp.int32)
    placement = (row_at == slot).astype(jnp.bfloat16)
    copy.wait()
    for k in range(count):
        part = placement[k * capacity : (k + 1) * capacity]
        packed[k][...] = jnp.dot(part, rows[...], preferred_element_type=jnp.float32).astype(
            jnp.bfloat16
        )


def pack(dest_row, points, group_count):
    row_count, feature_dim = points.shape
    capacity = row_count // group_count
    return pl.pallas_call(
        pack_kernel,
        out_shape=[jax.ShapeDtypeStruct((capacity, feature_dim), points.dtype)] * group_count,
        in_specs=[hbm(), hbm()],
        out_specs=[vmem()] * group_count,
        scratch_shapes=[
            pltpu.VMEM((1, row_count), jnp.int32),
            pltpu.VMEM((row_count, feature_dim), points.dtype),
            pltpu.SemaphoreType.DMA,
            pltpu.SemaphoreType.DMA,
        ],
        compiler_params=pltpu.CompilerParams(vmem_limit_bytes=vmem_limit),
        cost_estimate=cost(),
        name="pack",
    )(
        pltpu.with_memory_space_constraint(dest_row, pltpu.HBM),
        pltpu.with_memory_space_constraint(points, pltpu.HBM),
    )


def scaled_scores(table, half_norms, rows):
    dims = (((1,), (1,)), ((), ()))
    product = lax.dot_general(table, rows, dims, preferred_element_type=jnp.float32)
    return exponent_scale * (product - half_norms)


def softmax_terms(table, half_norms, rows, scores, tile):
    row_count = rows.shape[0]
    top = jnp.full((1, row_count), -jnp.inf, jnp.float32)
    total = jnp.zeros((1, row_count), jnp.float32)
    for start in range(0, table.shape[0], tile):
        at = slice(start, start + tile)
        block = scaled_scores(table[at, :], half_norms[at, :], rows)
        scores[at, :] = block
        higher = jnp.maximum(top, jnp.max(block, axis=0, keepdims=True))
        here = jnp.sum(jnp.exp2(block - higher), axis=0, keepdims=True)
        total = total * jnp.exp2(top - higher) + here
        top = higher
    return top, 1.0 / total


def gather_rows(parts, rows):
    start = 0
    for part in parts:
        if part is rows:
            return
        rows[start : start + part.shape[0], :] = part[...]
        start += part.shape[0]


def tile_sums(scores, top, inverse, rows):
    weights = (jnp.exp2(scores - top) * inverse).astype(jnp.bfloat16)
    sums = jnp.dot(weights, rows, preferred_element_type=jnp.float32)
    count = jnp.sum(weights.astype(jnp.float32), axis=1, keepdims=True)
    return sums, jnp.broadcast_to(count, (count.shape[0], lanes))


def at_tile(index, tile):
    return pl.ds(pl.multiple_of(index * tile, tile), tile)


def chip_place():
    member = lax.axis_index("member")
    core = member % 2
    return member // 2, core, member, member + 1 - 2 * core


def add_rows(table, half_norms, parts, rows, scores, sums, tile):
    feature_dim = table.shape[1]
    gather_rows(parts, rows)
    count = sum(part.shape[0] for part in parts)
    all_rows = rows[:count, :]
    scores = scores.at[:, :count]
    terms = softmax_terms(table, half_norms, all_rows, scores, tile)
    for index, out in sums:
        more, count = tile_sums(scores[at_tile(index, tile), :], *terms, all_rows)
        out[:, :feature_dim] += more
        out[:, feature_dim:] += count


def came_to(step, depth):
    level, core, _, _ = chip_place()
    return ((core == 0) & (level >= step)) | ((core == 1) & (level < depth - step))


def first_kernel(tile, depth, table_from, near, far, over, apart, *refs):
    table, keep, give, half_norms, arrivals, rows, scores = refs
    copies = []
    for index in range(arrivals.shape[0]):
        at = pl.ds(index * tile, tile)
        copies.append(pltpu.make_async_copy(table_from.at[at], table.at[at], arrivals.at[index]))
    for copy in copies:
        copy.start()
    keep[...] = jnp.zeros_like(keep)
    give[...] = jnp.zeros_like(give)
    for index, copy in enumerate(copies):
        copy.wait()
        at = slice(index * tile, (index + 1) * tile)
        block = table[at, :].astype(jnp.float32)
        half_norms[at, :] = 0.5 * jnp.sum(block * block, axis=1, keepdims=True)

    @pl.when(came_to(depth - 1, depth))
    def _():
        _, _, mine, other = chip_place()
        parts = (near, far, apart, over)
        add_rows(table, half_norms, parts, rows, scores, ((mine, keep), (other, give)), tile)


def own_kernel(tile, depth, table, half_norms, keep_in, give_in, near, far, over_near, *refs):
    came, (keep, give, rows, scores) = refs[:-4], refs[-4:]
    keep[...] = keep_in[...]
    give[...] = give_in[...]
    _, _, mine, other = chip_place()

    def add(*parts):
        add_rows(table, half_norms, parts, rows, scores, ((mine, keep), (other, give)), tile)

    end, here = came_to(depth - 1, depth), came_to(depth - 2, depth)

    @pl.when(end)
    def _():
        add(*came)

    @pl.when(here & jnp.logical_not(end))
    def _():
        add(near, far, over_near, *came)

    @pl.when(jnp.logical_not(here))
    def _():
        add(near, far)


def step_kernel(tile, depth, step, table, half_norms, keep_in, give_in, *refs):
    parts, (keep, give, rows, scores) = refs[:-4], refs[-4:]
    keep[...] = keep_in[...]
    give[...] = give_in[...]

    @pl.when(came_to(step, depth))
    def _():
        _, _, mine, other = chip_place()
        add_rows(table, half_norms, parts, rows, scores, ((mine, keep), (other, give)), tile)


def end_chip(depth):
    level = chip_place()[0]
    return (level == 0) | (level == depth - 1)


def base_kernel(tile, table, keep, *refs):
    parts, base = refs[:-1], refs[-1]
    feature_dim = table.shape[1]
    mine = chip_place()[2]
    start = 0
    for got in parts:
        rows = got.shape[0]
        span = slice(start, start + rows)
        old = table[pl.ds(pl.multiple_of(mine * tile + start, rows), rows), :].astype(jnp.float32)
        base[span, :feature_dim] = keep[span, :feature_dim] + got[:, :feature_dim] + old
        base[span, feature_dim:] = keep[span, feature_dim:] + got[:, feature_dim:] + 1.0
        start += rows


def refit_kernel(tile, depth, table, half_norms, base, came, passed, *refs):
    over_came, over_passed, refined, rows, scores, out, sent = refs
    feature_dim = table.shape[1]
    mine = chip_place()[2]
    end, here = end_chip(depth), came_to(1, depth)
    used = came.shape[0] + over_came.shape[0]

    @pl.when(end & here)
    def _():
        gather_rows((came, over_came), rows)
        rows[used:, :] = jnp.zeros_like(rows[used:, :])

    @pl.when(end & jnp.logical_not(here))
    def _():
        gather_rows((passed, over_passed), rows)
        rows[used:, :] = jnp.zeros_like(rows[used:, :])

    @pl.when(jnp.logical_not(end))
    def _():
        gather_rows((came, passed), rows)

    all_rows = rows[...]
    top, inverse = softmax_terms(table, half_norms, all_rows, scores, tile)
    lane = lax.broadcasted_iota(jnp.int32, inverse.shape, 1)
    terms = top, jnp.where(jnp.logical_not(end) | (lane < used), inverse, 0.0)
    half = tile // sent.shape[0]
    copies = []
    for index in range(sent.shape[0]):
        span = slice(index * half, (index + 1) * half)
        at = pl.ds(pl.multiple_of(mine * tile + index * half, half), half)
        sums, count = tile_sums(scores[at, :], *terms, all_rows)
        scale = 1.0 / (base[span, feature_dim : feature_dim + 1] + count[:, :1])
        out[span, :] = ((base[span, :feature_dim] + sums) * scale).astype(jnp.bfloat16)
        copies.append(pltpu.make_async_copy(out.at[span], refined.at[span], sent.at[index]))
        copies[-1].start()
    for copy in copies:
        copy.wait()


def cost(flops=1 << 20):
    return pl.CostEstimate(flops=flops, bytes_accessed=0, transcendentals=0)


def handoff(points, centroids, dest_group):
    group_count = lax.axis_size("group")
    member_count = lax.axis_size("member")
    depth = member_count // 2
    row_count, feature_dim = points.shape
    fine_count = centroids.shape[0]
    tile = fine_count // member_count

    def swap(x):
        return lax.ppermute(x, "member", [(i, i ^ 1) for i in range(member_count)])

    def along(x, moves):
        up = [(2 * z, 2 * to) for z, to in moves]
        down = [(2 * (depth - 1 - z) + 1, 2 * (depth - 1 - to) + 1) for z, to in moves]
        return lax.ppermute(x, "member", up + down)

    last = depth - 1
    apart = [(0, last - 1), (last - 1, last)]
    over = [(1, last)]
    beside = [(z, z + 1) for z in range(last)]

    sums_shape = jax.ShapeDtypeStruct((tile, feature_dim + lanes), jnp.float32)
    norms_shape = jax.ShapeDtypeStruct((fine_count, 1), jnp.float32)

    def kernel(body, out_shape, *operands, scratch=(), aliases={}, flops=1 << 28, specs=(), out_specs=None):
        return pl.pallas_call(
            body,
            out_shape=out_shape,
            in_specs=list(specs) + [vmem()] * (len(operands) - len(specs)),
            out_specs=out_specs or jax.tree.map(lambda _: vmem(), out_shape),
            scratch_shapes=scratch,
            input_output_aliases=aliases,
            compiler_params=pltpu.CompilerParams(vmem_limit_bytes=vmem_limit),
            cost_estimate=cost(flops),
            name=body.func.__name__,
        )(*operands)

    def scratch(rows):
        return [
            pltpu.VMEM((rows, feature_dim), jnp.bfloat16),
            pltpu.VMEM((fine_count, rows), jnp.float32),
        ]

    packed = pack(dest_group.reshape(1, row_count), points, group_count)
    fetched = [
        lax.ppermute(packed[k], "group", [(i, i ^ k) for i in range(group_count)])
        for k in reversed(range(1, group_count))
    ]
    near = join([packed[0], swap(packed[0])])
    apart_near, over_near = along(near, apart[1:]), along(near, over + apart[:1])
    first = join(fetched)
    slot_rows, far_rows = packed[0].shape[0], first.shape[0]
    apart_first = along(first, apart)
    halves = halve(first)
    swapped = [swap(half) for half in halves]
    second = join(swapped)
    apart_second = along(second, apart)
    over_first = along(join([first, second], spans=[(0, far_rows), (0, 2 * slot_rows)]), over)
    two_sums = [sums_shape, sums_shape]
    table, keep, give, half_norms = kernel(
        functools.partial(first_kernel, tile, depth),
        [like(centroids), *two_sums, norms_shape],
        pltpu.with_memory_space_constraint(centroids, pltpu.HBM),
        packed[0],
        first,
        over_near,
        apart_near,
        scratch=[pltpu.SemaphoreType.DMA((member_count,)), *scratch(row_count + 2 * near.shape[0])],
        flops=own_flops,
        specs=[hbm()],
    )

    def add(body, keep, give, *parts, flops=1 << 28):
        return kernel(
            body,
            two_sums,
            table,
            half_norms,
            keep,
            give,
            *parts,
            scratch=scratch(sum(part.shape[0] for part in parts)),
            aliases={2: 0, 3: 1},
            flops=flops,
        )

    beside_first = along(pick(depth, first, apart_first, keep, pick_flops), beside)
    beside_second = along(pick(depth, second, apart_second, keep), beside)
    beside_near = along(pick(depth, near, over_near, keep), beside)
    over_second = along(join([second], spans=[(2 * slot_rows, far_rows)]), over)
    own_body = functools.partial(own_kernel, tile, depth)
    keep, give = add(own_body, keep, give, packed[0], first, over_near, apart_first, apart_second)
    over_body = functools.partial(step_kernel, tile, depth, last)
    keep, give = add(over_body, keep, give, over_first)
    beside_body = functools.partial(step_kernel, tile, depth, 1)
    keep, give = add(beside_body, keep, give, beside_first, flops=beside_flops)
    keep, give = add(beside_body, keep, give, beside_second)
    base = kernel(
        functools.partial(base_kernel, tile),
        sums_shape,
        table,
        keep,
        swap(give[: tile // 2]),
        swap(give[tile // 2 :]),
        flops=1 << 20,
    )
    over_last = join([over_second], keep, flops=over_flops)
    beside_last = join([beside_near], keep, flops=last_flops)
    return kernel(
        functools.partial(refit_kernel, tile, depth),
        jax.ShapeDtypeStruct((tile, feature_dim), jnp.bfloat16),
        table,
        half_norms,
        base,
        beside_last,
        swap(beside_last),
        over_last,
        swap(over_last),
        scratch=scratch(2 * near.shape[0])
        + [pltpu.VMEM((tile, feature_dim), jnp.bfloat16), pltpu.SemaphoreType.DMA((2,))],
        out_specs=hbm(),
    )


def solution(mesh):
    def local(points, centroids, dest_group):
        groups, members = mesh.shape["group"], mesh.shape["member"]
        if groups * (points.shape[0] // 4) == points.shape[0] and members // 2 == 4:
            return handoff(points, centroids, dest_group)
        return general(points, centroids, dest_group)

    return jax.shard_map(
        local,
        mesh=mesh,
        in_specs=(P(("group", "member"), None), P("group", None), P(("group", "member"), None)),
        out_specs=P(("group", "member"), None),
        check_vma=False,
    )
```

```python
import functools
import math

import jax
import jax.numpy as jnp
from jax import lax
from jax.experimental import pallas as pl
from jax.experimental.pallas import tpu as pltpu
from jax.sharding import PartitionSpec as P

score_scale = 0.15
lanes = 128
exponent_scale = score_scale * math.log2(math.e)
pick_flops = 1 << 30
own_flops = 1 << 31
beside_flops = 1 << 28
over_flops = 1 << 32
last_flops = 1 << 26
vmem_limit = 20 * 1024 * 1024


def general(points, centroids, dest_group):
    group_count = lax.axis_size("group")
    member_count = lax.axis_size("member")
    point_rows = points.shape[0]
    capacity = point_rows // 4
    feature_dim = points.shape[1]
    fine_count = centroids.shape[0]
    destination = dest_group[:, 0]
    in_group = (destination[:, None] == jnp.arange(group_count, dtype=jnp.int32)[None, :]).astype(
        jnp.int32
    )
    earlier = jnp.cumsum(in_group, axis=0) - in_group
    own_rank = jnp.sum(earlier * in_group, axis=1)
    slot_index = destination * capacity + own_rank
    placement = (
        jnp.arange(group_count * capacity, dtype=jnp.int32)[:, None] == slot_index[None, :]
    ).astype(jnp.bfloat16)
    packed = jnp.dot(placement, points, preferred_element_type=jnp.float32).astype(jnp.bfloat16)
    packed = packed.reshape(group_count, capacity, feature_dim)
    slot_flags = jnp.dot(
        placement, jnp.ones((point_rows, 1), jnp.bfloat16), preferred_element_type=jnp.float32
    )
    slot_flags = slot_flags.astype(jnp.bfloat16).reshape(group_count, capacity, 1)
    centroid_f = centroids.astype(jnp.float32)
    centroid_norms = jnp.sum(centroid_f * centroid_f, axis=1)
    arrived, marks = (
        lax.all_to_all(packed, "group", split_axis=0, concat_axis=0, tiled=True),
        lax.all_to_all(slot_flags, "group", split_axis=0, concat_axis=0, tiled=True),
    )
    rows = arrived.reshape(-1, feature_dim)
    scores = score_scale * (
        jnp.dot(rows, centroids.T, preferred_element_type=jnp.float32)
        - 0.5 * centroid_norms[None, :]
    )
    weights = jax.nn.softmax(scores, axis=-1) * marks.reshape(-1, 1).astype(jnp.float32)
    responsibility = weights.astype(jnp.bfloat16).reshape(
        arrived.shape[0], arrived.shape[1], fine_count
    )
    all_rows = arrived.reshape(-1, feature_dim)
    all_weights = responsibility.reshape(-1, fine_count)
    weighted = jnp.dot(all_weights.T, all_rows, preferred_element_type=jnp.float32)
    soft_counts = jnp.dot(
        jnp.ones((1, all_weights.shape[0]), jnp.bfloat16),
        all_weights,
        preferred_element_type=jnp.float32,
    )[0]
    member_index = lax.axis_index("member")
    tile_sums, tile_counts = (
        lax.psum_scatter(weighted, "member", scatter_dimension=0, tiled=True),
        lax.psum_scatter(soft_counts, "member", scatter_dimension=0, tiled=True),
    )
    tile_rows = fine_count // member_count
    old_tile = lax.dynamic_slice_in_dim(centroid_f, member_index * tile_rows, tile_rows, 0)
    refined = ((tile_sums + old_tile) / (tile_counts + 1.0)[:, None]).astype(jnp.bfloat16)
    return refined


def vmem():
    return pl.BlockSpec(memory_space=pltpu.VMEM)


def hbm():
    return pl.BlockSpec(memory_space=pltpu.HBM)


def unread():
    return pl.BlockSpec(memory_space=pl.ANY)


def like(x):
    return jax.ShapeDtypeStruct(x.shape, x.dtype)


def join_kernel(after_n, spans, *refs):
    out, start = refs[-1], 0
    for (low, high), part in zip(spans, refs[after_n:-1]):
        out[start : start + high - low, :] = part[low:high, :]
        start += high - low


def join(parts, *after, flops=1 << 20, spans=None):
    spans = spans or [(0, part.shape[0]) for part in parts]
    rows = sum(high - low for low, high in spans)
    return pl.pallas_call(
        functools.partial(join_kernel, len(after), spans),
        out_shape=jax.ShapeDtypeStruct((rows, parts[0].shape[1]), parts[0].dtype),
        in_specs=[unread()] * len(after) + [vmem()] * len(parts),
        out_specs=vmem(),
        compiler_params=pltpu.CompilerParams(vmem_limit_bytes=vmem_limit),
        cost_estimate=cost(flops),
        name="join",
    )(*after, *parts)


def halve_kernel(whole, upper, lower):
    upper[...] = whole[: upper.shape[0], :]
    lower[...] = whole[upper.shape[0] :, :]


def halve(whole):
    half = jax.ShapeDtypeStruct((whole.shape[0] // 2, whole.shape[1]), whole.dtype)
    return pl.pallas_call(
        halve_kernel,
        out_shape=[half, half],
        in_specs=[vmem()],
        out_specs=[vmem(), vmem()],
        compiler_params=pltpu.CompilerParams(vmem_limit_bytes=vmem_limit),
        cost_estimate=cost(),
        name="halve",
    )(whole)


def pick_kernel(depth, own, came, after, out):
    level, core, _, _ = chip_place()
    forwards = ((core == 0) & (level == depth - 2)) | ((core == 1) & (level == 1))

    @pl.when(forwards)
    def _():
        out[...] = came[...]

    @pl.when(jnp.logical_not(forwards))
    def _():
        out[...] = own[...]


def pick(depth, own, came, after, flops=1 << 20):
    return pl.pallas_call(
        functools.partial(pick_kernel, depth),
        out_shape=like(own),
        in_specs=[vmem(), vmem(), unread()],
        out_specs=vmem(),
        compiler_params=pltpu.CompilerParams(vmem_limit_bytes=vmem_limit),
        cost_estimate=cost(flops),
        name="pick",
    )(own, came, after)


def pack_kernel(dest_from, points, *refs):
    packed, (dest, rows, dest_arrival, arrival) = refs[:-4], refs[-4:]
    dest_copy = pltpu.make_async_copy(dest_from, dest, dest_arrival)
    copy = pltpu.make_async_copy(points, rows, arrival)
    copy.start()
    dest_copy.start()
    count = len(packed)
    row_count = rows.shape[0]
    capacity = row_count // count
    dest_copy.wait()
    apart = jnp.bitwise_xor(dest[...], lax.axis_index("group"))
    named = lax.broadcasted_iota(jnp.int32, (8, row_count), 0) == apart
    row_at = lax.broadcasted_iota(jnp.int32, (row_count, row_count), 0)
    col_at = lax.broadcasted_iota(jnp.int32, (row_count, row_count), 1)
    before = (row_at < col_at).astype(jnp.bfloat16)
    named = named.astype(jnp.float32)
    earlier = jnp.dot(named.astype(jnp.bfloat16), before, preferred_element_type=jnp.float32)
    rank = jnp.sum(earlier * named, axis=0, keepdims=True)
    slot = apart * capacity + rank.astype(jnp.int32)
    placement = (row_at == slot).astype(jnp.bfloat16)
    copy.wait()
    for k in range(count):
        part = placement[k * capacity : (k + 1) * capacity]
        packed[k][...] = jnp.dot(part, rows[...], preferred_element_type=jnp.float32).astype(
            jnp.bfloat16
        )


def pack(dest_row, points, group_count):
    row_count, feature_dim = points.shape
    capacity = row_count // group_count
    return pl.pallas_call(
        pack_kernel,
        out_shape=[jax.ShapeDtypeStruct((capacity, feature_dim), points.dtype)] * group_count,
        in_specs=[hbm(), hbm()],
        out_specs=[vmem()] * group_count,
        scratch_shapes=[
            pltpu.VMEM((1, row_count), jnp.int32),
            pltpu.VMEM((row_count, feature_dim), points.dtype),
            pltpu.SemaphoreType.DMA,
            pltpu.SemaphoreType.DMA,
        ],
        compiler_params=pltpu.CompilerParams(vmem_limit_bytes=vmem_limit),
        cost_estimate=cost(),
        name="pack",
    )(
        pltpu.with_memory_space_constraint(dest_row, pltpu.HBM),
        pltpu.with_memory_space_constraint(points, pltpu.HBM),
    )


def scaled_scores(table, half_norms, rows):
    dims = (((1,), (1,)), ((), ()))
    product = lax.dot_general(table, rows, dims, preferred_element_type=jnp.float32)
    return exponent_scale * (product - half_norms)


def softmax_terms(table, half_norms, rows, scores, tile):
    row_count = rows.shape[0]
    top = jnp.full((1, row_count), -jnp.inf, jnp.float32)
    total = jnp.zeros((1, row_count), jnp.float32)
    for start in range(0, table.shape[0], tile):
        at = slice(start, start + tile)
        block = scaled_scores(table[at, :], half_norms[at, :], rows)
        scores[at, :] = block
        higher = jnp.maximum(top, jnp.max(block, axis=0, keepdims=True))
        here = jnp.sum(jnp.exp2(block - higher), axis=0, keepdims=True)
        total = total * jnp.exp2(top - higher) + here
        top = higher
    return top, 1.0 / total


def gather_rows(parts, rows):
    start = 0
    for part in parts:
        if part is rows:
            return
        rows[start : start + part.shape[0], :] = part[...]
        start += part.shape[0]


def tile_sums(scores, top, inverse, rows):
    weights = (jnp.exp2(scores - top) * inverse).astype(jnp.bfloat16)
    sums = jnp.dot(weights, rows, preferred_element_type=jnp.float32)
    count = jnp.sum(weights.astype(jnp.float32), axis=1, keepdims=True)
    return sums, jnp.broadcast_to(count, (count.shape[0], lanes))


def at_tile(index, tile):
    return pl.ds(pl.multiple_of(index * tile, tile), tile)


def chip_place():
    member = lax.axis_index("member")
    core = member % 2
    return member // 2, core, member, member + 1 - 2 * core


def add_rows(table, half_norms, parts, rows, scores, sums, tile):
    feature_dim = table.shape[1]
    gather_rows(parts, rows)
    count = sum(part.shape[0] for part in parts)
    all_rows = rows[:count, :]
    scores = scores.at[:, :count]
    terms = softmax_terms(table, half_norms, all_rows, scores, tile)
    for index, out in sums:
        more, count = tile_sums(scores[at_tile(index, tile), :], *terms, all_rows)
        out[:, :feature_dim] += more
        out[:, feature_dim:] += count


def came_to(step, depth):
    level, core, _, _ = chip_place()
    return ((core == 0) & (level >= step)) | ((core == 1) & (level < depth - step))


def first_kernel(tile, depth, table_from, near, far, over, apart, *refs):
    table, keep, give, half_norms, arrivals, rows, scores = refs
    copies = []
    for index in range(arrivals.shape[0]):
        at = pl.ds(index * tile, tile)
        copies.append(pltpu.make_async_copy(table_from.at[at], table.at[at], arrivals.at[index]))
    for copy in copies:
        copy.start()
    keep[...] = jnp.zeros_like(keep)
    give[...] = jnp.zeros_like(give)
    for index, copy in enumerate(copies):
        copy.wait()
        at = slice(index * tile, (index + 1) * tile)
        block = table[at, :].astype(jnp.float32)
        half_norms[at, :] = 0.5 * jnp.sum(block * block, axis=1, keepdims=True)

    @pl.when(came_to(depth - 1, depth))
    def _():
        _, _, mine, other = chip_place()
        parts = (near, far, apart, over)
        add_rows(table, half_norms, parts, rows, scores, ((mine, keep), (other, give)), tile)


def own_kernel(tile, depth, table, half_norms, keep_in, give_in, near, far, over_near, *refs):
    came, (keep, give, rows, scores) = refs[:-4], refs[-4:]
    keep[...] = keep_in[...]
    give[...] = give_in[...]
    _, _, mine, other = chip_place()

    def add(*parts):
        add_rows(table, half_norms, parts, rows, scores, ((mine, keep), (other, give)), tile)

    end, here = came_to(depth - 1, depth), came_to(depth - 2, depth)

    @pl.when(end)
    def _():
        add(*came)

    @pl.when(here & jnp.logical_not(end))
    def _():
        add(near, far, over_near, *came)

    @pl.when(jnp.logical_not(here))
    def _():
        add(near, far)


def step_kernel(tile, depth, step, table, half_norms, keep_in, give_in, *refs):
    parts, (keep, give, rows, scores) = refs[:-4], refs[-4:]
    keep[...] = keep_in[...]
    give[...] = give_in[...]

    @pl.when(came_to(step, depth))
    def _():
        _, _, mine, other = chip_place()
        add_rows(table, half_norms, parts, rows, scores, ((mine, keep), (other, give)), tile)


def end_chip(depth):
    level = chip_place()[0]
    return (level == 0) | (level == depth - 1)


def base_kernel(tile, table, keep, *refs):
    parts, base = refs[:-1], refs[-1]
    feature_dim = table.shape[1]
    mine = chip_place()[2]
    start = 0
    for got in parts:
        rows = got.shape[0]
        span = slice(start, start + rows)
        old = table[pl.ds(pl.multiple_of(mine * tile + start, rows), rows), :].astype(jnp.float32)
        base[span, :feature_dim] = keep[span, :feature_dim] + got[:, :feature_dim] + old
        base[span, feature_dim:] = keep[span, feature_dim:] + got[:, feature_dim:] + 1.0
        start += rows


def refit_kernel(tile, depth, table, half_norms, base, came, passed, *refs):
    over_came, over_passed, refined, rows, scores, out, sent = refs
    feature_dim = table.shape[1]
    mine = chip_place()[2]
    end, here = end_chip(depth), came_to(1, depth)

    @pl.when(end & here)
    def _():
        gather_rows((came, over_came), rows)

    @pl.when(end & jnp.logical_not(here))
    def _():
        gather_rows((passed, over_passed), rows)

    @pl.when(jnp.logical_not(end))
    def _():
        gather_rows((came, passed), rows)

    all_rows = rows[...]
    terms = softmax_terms(table, half_norms, all_rows, scores, tile)
    half = tile // sent.shape[0]
    copies = []
    for index in range(sent.shape[0]):
        span = slice(index * half, (index + 1) * half)
        at = pl.ds(pl.multiple_of(mine * tile + index * half, half), half)
        sums, count = tile_sums(scores[at, :], *terms, all_rows)
        scale = 1.0 / (base[span, feature_dim : feature_dim + 1] + count[:, :1])
        out[span, :] = ((base[span, :feature_dim] + sums) * scale).astype(jnp.bfloat16)
        copies.append(pltpu.make_async_copy(out.at[span], refined.at[span], sent.at[index]))
        copies[-1].start()
    for copy in copies:
        copy.wait()


def cost(flops=1 << 20):
    return pl.CostEstimate(flops=flops, bytes_accessed=0, transcendentals=0)


def handoff(points, centroids, dest_group):
    group_count = lax.axis_size("group")
    member_count = lax.axis_size("member")
    depth = member_count // 2
    row_count, feature_dim = points.shape
    fine_count = centroids.shape[0]
    tile = fine_count // member_count

    def swap(x):
        return lax.ppermute(x, "member", [(i, i ^ 1) for i in range(member_count)])

    def along(x, moves):
        up = [(2 * z, 2 * to) for z, to in moves]
        down = [(2 * (depth - 1 - z) + 1, 2 * (depth - 1 - to) + 1) for z, to in moves]
        return lax.ppermute(x, "member", up + down)

    last = depth - 1
    apart = [(0, last - 1), (last - 1, last)]
    over = [(1, last)]
    beside = [(z, z + 1) for z in range(last)]

    sums_shape = jax.ShapeDtypeStruct((tile, feature_dim + lanes), jnp.float32)
    norms_shape = jax.ShapeDtypeStruct((fine_count, 1), jnp.float32)

    def kernel(body, out_shape, *operands, scratch=(), aliases={}, flops=1 << 28, specs=(), out_specs=None):
        return pl.pallas_call(
            body,
            out_shape=out_shape,
            in_specs=list(specs) + [vmem()] * (len(operands) - len(specs)),
            out_specs=out_specs or jax.tree.map(lambda _: vmem(), out_shape),
            scratch_shapes=scratch,
            input_output_aliases=aliases,
            compiler_params=pltpu.CompilerParams(vmem_limit_bytes=vmem_limit),
            cost_estimate=cost(flops),
            name=body.func.__name__,
        )(*operands)

    def scratch(rows):
        return [
            pltpu.VMEM((rows, feature_dim), jnp.bfloat16),
            pltpu.VMEM((fine_count, rows), jnp.float32),
        ]

    packed = pack(dest_group.reshape(1, row_count), points, group_count)
    fetched = [
        lax.ppermute(packed[k], "group", [(i, i ^ k) for i in range(group_count)])
        for k in reversed(range(1, group_count))
    ]
    near = join([packed[0], swap(packed[0])])
    apart_near, over_near = along(near, apart[1:]), along(near, over + apart[:1])
    first = join(fetched)
    slot_rows, far_rows = packed[0].shape[0], first.shape[0]
    apart_first = along(first, apart)
    halves = halve(first)
    swapped = [swap(half) for half in halves]
    second = join(swapped)
    apart_second = along(second, apart)
    over_first = along(join([first, second], spans=[(0, far_rows), (0, slot_rows)]), over)
    two_sums = [sums_shape, sums_shape]
    table, keep, give, half_norms = kernel(
        functools.partial(first_kernel, tile, depth),
        [like(centroids), *two_sums, norms_shape],
        pltpu.with_memory_space_constraint(centroids, pltpu.HBM),
        packed[0],
        first,
        over_near,
        apart_near,
        scratch=[pltpu.SemaphoreType.DMA((member_count,)), *scratch(row_count + 2 * near.shape[0])],
        flops=own_flops,
        specs=[hbm()],
    )

    def add(body, keep, give, *parts, flops=1 << 28):
        return kernel(
            body,
            two_sums,
            table,
            half_norms,
            keep,
            give,
            *parts,
            scratch=scratch(sum(part.shape[0] for part in parts)),
            aliases={2: 0, 3: 1},
            flops=flops,
        )

    beside_first = along(pick(depth, first, apart_first, keep, pick_flops), beside)
    beside_second = along(pick(depth, second, apart_second, keep), beside)
    beside_near = along(pick(depth, near, over_near, keep), beside)
    over_second = along(join([second], spans=[(slot_rows, far_rows)]), over)
    own_body = functools.partial(own_kernel, tile, depth)
    keep, give = add(own_body, keep, give, packed[0], first, over_near, apart_first, apart_second)
    over_body = functools.partial(step_kernel, tile, depth, last)
    keep, give = add(over_body, keep, give, over_first)
    beside_body = functools.partial(step_kernel, tile, depth, 1)
    keep, give = add(beside_body, keep, give, beside_first, flops=beside_flops)
    keep, give = add(beside_body, keep, give, beside_second)
    base = kernel(
        functools.partial(base_kernel, tile),
        sums_shape,
        table,
        keep,
        swap(give[: tile // 2]),
        swap(give[tile // 2 :]),
        flops=1 << 20,
    )
    over_last = join([over_second], keep, flops=over_flops)
    beside_last = join([beside_near], keep, flops=last_flops)
    return kernel(
        functools.partial(refit_kernel, tile, depth),
        jax.ShapeDtypeStruct((tile, feature_dim), jnp.bfloat16),
        table,
        half_norms,
        base,
        beside_last,
        swap(beside_last),
        over_last,
        swap(over_last),
        scratch=scratch(2 * near.shape[0])
        + [pltpu.VMEM((tile, feature_dim), jnp.bfloat16), pltpu.SemaphoreType.DMA((2,))],
        out_specs=hbm(),
    )


def solution(mesh):
    def local(points, centroids, dest_group):
        groups, members = mesh.shape["group"], mesh.shape["member"]
        if groups * (points.shape[0] // 4) == points.shape[0] and members // 2 == 4:
            return handoff(points, centroids, dest_group)
        return general(points, centroids, dest_group)

    return jax.shard_map(
        local,
        mesh=mesh,
        in_specs=(P(("group", "member"), None), P("group", None), P(("group", "member"), None)),
        out_specs=P(("group", "member"), None),
        check_vma=False,
    )
```
